128 devices in a mesh: band: 8 (over y_hi, x), led: 4 (over z), pencil: 4 (over y_lo, core).
Axes of the slice: x: 4, y: 4 (y_hi: 2, y_lo: 2; y = y_hi * 2 + y_lo), z: 4, core: 2. Of those that a mesh axis runs over, the one named last changes fastest.
Arguments:
- spectrum: float32 [128, 64, 2, 8192], P(('band', 'led', 'pencil')), may hold values from -6 to 6
- pupil: float32 [2, 2048, 2048], P(None, None, ('band', 'pencil')), may hold values from -5 to 5
- measured: float32 [8, 2048, 2048], P('led', ('band', 'pencil')), may hold values from 0.05 to 4
- offsets: int32 [8, 2], replicated, may hold values from 0 to 6144
Outputs:
- spectrum_grad: float32 [128, 64, 2, 8192], P(('band', 'led', 'pencil'))
- pupil_grad: float32 [2, 2048, 2048], P(None, None, ('band', 'pencil'))
The draws below stay inside these ranges and needn't reach their ends.
Inputs may be any that keep to these rules, and one draw needn't show every extreme that they name: offsets[l, 0] and offsets[l, 1] are the first row and first column of LED l's window, which lies inside the spectrum.
All inputs are finite; a program needn't handle non-finite values.
Results may differ from the reference program's by a relative error of at most 0.008.
Values may be sent and summed in bfloat16 or wider, within the bound.
A program may use at most 128 MiB of HBM per device.

```python
import math
import jax
import jax.numpy as jnp
from jax import lax

S = 8192
W = 2048
L = 8
ROWS_DEV = 64
DEVICES = 128


def plant(array, key, least, high):
    place = [jax.random.randint(jax.random.fold_in(key, axis), (), 0, length) for axis, length in enumerate(array.shape)]
    main_axis = array.shape.index(max(array.shape))
    beside = place[:main_axis] + [(place[main_axis] + 1) % array.shape[main_axis]] + place[main_axis + 1:]
    return array.at[tuple(place)].set(least).at[tuple(beside)].set(high)


def level_of(key, shape, pieces, smallest, largest):
    def one(dim, blocks):
        steps = jax.random.uniform(jax.random.fold_in(jax.random.fold_in(key, 6), dim), (blocks,), jnp.float32, smallest / len(pieces), largest / len(pieces))
        return jnp.repeat(jnp.exp(steps), shape[dim] // blocks).reshape((-1,) + (1,) * (len(shape) - dim - 1))

    gain = one(*pieces[0])
    for cut in pieces[1:]:
        gain = gain * one(*cut)
    return gain


def bell_draw(own_key, dims, spread, most, shards=(), dtype=jnp.bfloat16):
    array = jax.random.normal(own_key, dims, jnp.float32) * spread
    if len(shards) > 0:
        array = level_of(own_key, dims, shards, -0.22, 0.18) * array
    return jnp.clip(array, min=-most, max=most).astype(dtype)


def setup_inputs(seed: int = 0) -> dict:
    keys = jax.random.split(jax.random.key(seed), 5)
    spectrum = bell_draw(keys[0], (DEVICES, ROWS_DEV, 2, S), 1.0, 6.0, ((0, 128),), jnp.float32)
    pupil = bell_draw(keys[1], (2, W, W), 0.7, 5.0, ((2, 32),), jnp.float32)
    measured = jnp.clip(jnp.exp(math.log(4.0) - 4.3820266 * jax.random.uniform(keys[2], (L, W, W), jnp.float32) ** level_of(keys[2], (L, W, W), ((0, 4), (1, 32)), -0.2, 0.2)), 0.05, 4.0)
    offsets = plant(jax.random.randint(keys[3], (L, 2), 0, S - W + 1), jax.random.fold_in(keys[3], 1), 0, S - W).astype(jnp.int32)
    return {"spectrum": spectrum, "pupil": pupil, "measured": measured, "offsets": offsets}


def make_tables(size):
    rows = lax.broadcasted_iota(jnp.int32, (size, size), 0)
    cols = lax.broadcasted_iota(jnp.int32, (size, size), 1)
    phase = (rows * cols % size).astype(jnp.float32) * (2.0 * math.pi / size)
    return (jnp.cos(phase).astype(jnp.bfloat16), jnp.sin(phase).astype(jnp.bfloat16))

def contract_first(left, right):
    return lax.dot_general(left, right, (((0,), (0,)), ((), ())), preferred_element_type=jnp.float32)

def reference(spectrum, pupil, measured, offsets):
    devices = spectrum.shape[0]
    rows_dev = spectrum.shape[1]
    extent = spectrum.shape[3]
    window = pupil.shape[1]
    led_count = offsets.shape[0]
    full_rows = jnp.transpose(spectrum, (1, 0, 2, 3)).reshape(extent, 2, extent)
    cosine, sine_table = make_tables(window)
    pupil_re = pupil[0]
    pupil_im = pupil[1]
    spec_grad = jnp.zeros((extent, 2, extent), jnp.float32)
    pupil_total = jnp.zeros((2, window, window), jnp.float32)
    zero_index = jnp.int32(0)
    for led_id in range(led_count):
        row_start = offsets[led_id, 0].astype(jnp.int32)
        col_start = offsets[led_id, 1].astype(jnp.int32)
        win = lax.dynamic_slice(full_rows, (row_start, zero_index, col_start), (window, 2, window)).astype(jnp.bfloat16)
        win_re = win[:, 0, :]
        win_im = win[:, 1, :]
        prod_re = (win_re * pupil_re - win_im * pupil_im).astype(jnp.bfloat16)
        prod_im = (win_re * pupil_im + win_im * pupil_re).astype(jnp.bfloat16)
        half_re = (contract_first(prod_re, cosine) - contract_first(prod_im, sine_table)).astype(jnp.bfloat16)
        half_im = (contract_first(prod_im, cosine) + contract_first(prod_re, sine_table)).astype(jnp.bfloat16)
        field_re = (contract_first(half_re, cosine) - contract_first(half_im, sine_table)) / window
        field_im = (contract_first(half_im, cosine) + contract_first(half_re, sine_table)) / window
        amplitude = jnp.sqrt(field_re * field_re + field_im * field_im)
        factor = 1.0 - jnp.sqrt(measured[led_id]) / jnp.maximum(amplitude, 0.5)
        resid_re = (field_re * factor).astype(jnp.bfloat16)
        resid_im = (field_im * factor).astype(jnp.bfloat16)
        back_re = (jnp.dot(resid_re, cosine, preferred_element_type=jnp.float32) + jnp.dot(resid_im, sine_table, preferred_element_type=jnp.float32)).astype(jnp.bfloat16)
        back_im = (jnp.dot(resid_im, cosine, preferred_element_type=jnp.float32) - jnp.dot(resid_re, sine_table, preferred_element_type=jnp.float32)).astype(jnp.bfloat16)
        grad_re = (contract_first(cosine, back_re) + contract_first(sine_table, back_im)) / window
        grad_im = (contract_first(cosine, back_im) - contract_first(sine_table, back_re)) / window
        term_re = (pupil_re * grad_re + pupil_im * grad_im).astype(jnp.bfloat16).astype(jnp.float32)
        term_im = (pupil_re * grad_im - pupil_im * grad_re).astype(jnp.bfloat16).astype(jnp.float32)
        current = lax.dynamic_slice(spec_grad, (row_start, zero_index, col_start), (window, 2, window))
        current = current + jnp.stack([term_re, term_im], axis=1)
        spec_grad = lax.dynamic_update_slice(spec_grad, current, (row_start, zero_index, col_start))
        pupil_total = pupil_total + jnp.stack([win_re * grad_re + win_im * grad_im, win_re * grad_im - win_im * grad_re])
    spectrum_grad = jnp.transpose(spec_grad.reshape(rows_dev, devices, 2, extent), (1, 0, 2, 3))
    return (spectrum_grad, pupil_total)
```

```python
import functools
import math

import jax
import jax.numpy as jnp
import ml_dtypes
import numpy as np
from jax import lax
from jax.experimental import pallas as pl
from jax.experimental.pallas import tpu as pltpu
from jax.sharding import PartitionSpec as P

W = 2048
Q = W // 4
LANES = 128
STRIPS = 16
DEVICES = 128
BLOCKS = 32
GROUPS = 4
PER = 2
LEDS = 8
MESH = pl.DeviceIdType.MESH
F32 = jnp.float32
BF16 = jnp.bfloat16


def trig(left, right):
    phase = (np.outer(left, right) % W).astype(np.float64) * (2.0 * math.pi / W)
    return np.cos(phase).astype(np.float32), np.sin(phase).astype(np.float32)


@functools.lru_cache(maxsize=None)
def tables():
    low = np.arange(Q)
    rows_fwd, cols_fwd, cols_back, rows_back = [], [], [], []
    for part in range(4):
        j = (4 * np.arange(32)[:, None] + part + LANES * np.arange(STRIPS)[None, :]).reshape(-1)
        c, s = trig(low, j)
        rows_fwd.append(np.concatenate([c, s], axis=1))
        rows_back.append(np.concatenate([c.T, s.T], axis=1) / W)
        n = 4 * low + part
        c, s = trig(low, n)
        c, s = c.reshape(8, 64, Q), s.reshape(8, 64, Q)
        re = np.concatenate([c, s], axis=2)
        im = np.concatenate([-s, c], axis=2)
        both = np.stack([re, im], axis=1).reshape(2 * Q, 2 * Q)
        cols_fwd.append(both / W)
        cols_back.append(both.T)
    return tuple(np.stack(t).astype(ml_dtypes.bfloat16) for t in (rows_fwd, cols_fwd, cols_back, rows_back))


def lane_id(rows):
    return lax.broadcasted_iota(jnp.int32, (rows, LANES), 1)


def swap(x):
    return pltpu.roll(x, 64, 1)


def position():
    return lax.axis_index("band"), lax.axis_index("led"), lax.axis_index("pencil")


def cut_kernel(off, x, out):
    band, led, pencil = position()
    me = band * 16 + led * 4 + pencil
    lane = lane_id(STRIPS)
    half = lane < 64

    def one(l, carry):
        first = (off[l, 0] - me + (DEVICES - 1)) >> 7
        col = off[l, 1]
        tile, within = col >> 7, col & 127
        keep = lane < LANES - within
        turn = (LANES - within) & 127

        def load(k, part):
            at = first * LANES + 2 * jnp.minimum(tile + k, 63) + part
            return pltpu.roll(x[pl.ds(at, STRIPS, stride=LANES), :], turn, 1)

        re, im = load(0, 0), load(0, 1)
        for k in range(16):
            next_re, next_im = load(k + 1, 0), load(k + 1, 1)
            a = jnp.where(keep, re, next_re)
            b = jnp.where(keep, im, next_im)
            slot = (l >> 1) * BLOCKS + 2 * k
            out[slot, l & 1] = jnp.where(half, a, swap(b)).astype(BF16)
            out[slot + 1, l & 1] = jnp.where(half, swap(a), b).astype(BF16)
            re, im = next_re, next_im
        return carry

    lax.fori_loop(0, LEDS, one, 0)


def add_kernel(off, terms, out):
    band, led, pencil = position()
    me = band * 16 + led * 4 + pencil
    lane = lane_id(STRIPS)
    half = lane < 64

    def clear(i, carry):
        out[pl.ds(pl.multiple_of(i * 256, 256), 256), :] = jnp.zeros((256, LANES), F32)
        return carry

    lax.fori_loop(0, out.shape[0] // 256, clear, 0)

    def one(l, carry):
        first = (off[l, 0] - me + (DEVICES - 1)) >> 7
        col = off[l, 1]
        tile, within = col >> 7, col & 127
        low = lane < within

        def place(k, part):
            return pl.ds(first * LANES + 2 * jnp.minimum(tile + k, 63) + part, STRIPS, stride=LANES)

        zero = jnp.zeros((STRIPS, LANES), F32)
        last = (zero, zero)
        values = []
        for k in range(16):
            slot = (l >> 1) * BLOCKS + 2 * k
            a = terms[slot, l & 1].astype(F32)
            b = terms[slot + 1, l & 1].astype(F32)
            now = (
                pltpu.roll(jnp.where(half, a, swap(b)), within, 1),
                pltpu.roll(jnp.where(half, swap(a), b), within, 1),
            )
            values.append([out[place(k, p), :] + jnp.where(low, last[p], now[p]) for p in range(2)])
            last = now
        for k in range(16):
            for p in range(2):
                out[place(k, p), :] = values[k][p]
        for p in range(2):
            out[place(16, p), :] = out[place(16, p), :] + jnp.where(low, last[p], zero)
        return carry

    lax.fori_loop(0, LEDS, one, 0)


def core_kernel(
    off, send1, pup, meas, h1, h2, h3, h4, recv4, pgout,
    t1, t2, t3, t4, recv1, pup_r, pup_i, tmp_r, tmp_i, perm, smq, x1, ys, send2, recv2, xq, rq, zs,
    send3, recv3, wg, send4, pg, pg16, rsr, agr,
    tsem, s1, r1, s2, r2, s3, r3, s4, r4, s5, r5, s6, r6,
):
    band, led, pencil = position()
    me = band * 16 + led * 4 + pencil
    block = band * 4 + pencil
    slot_me = led * BLOCKS + block
    sgn = jnp.where(lane_id(1) < 64, -1.0, 1.0).astype(F32)

    def device(d):
        return {"band": d >> 4, "led": (d >> 2) & 3, "pencil": d & 3}

    def plane(b):
        return {"band": b >> 2, "led": led, "pencil": b & 3}

    fetch = [pltpu.make_async_copy(h, t, tsem.at[i]) for i, (h, t) in enumerate(((h1, t1), (h2, t2), (h3, t3), (h4, t4)))]
    for f in fetch:
        f.start()

    barrier = pltpu.get_barrier_semaphore()

    def greet(i, c):
        pl.semaphore_signal(barrier, inc=1, device_id=device((me + i) & 127), device_id_type=MESH)
        return c

    lax.fori_loop(1, DEVICES, greet, 0)
    pl.semaphore_wait(barrier, DEVICES - 1)

    def start1(i, c):
        d = (me + i) & 127
        slot = ((d >> 2) & 3) * BLOCKS + (d >> 4) * 4 + (d & 3)
        pltpu.make_async_remote_copy(
            src_ref=send1.at[slot], dst_ref=recv1.at[me], send_sem=s1, recv_sem=r1, device_id=device(d), device_id_type=MESH
        ).start()
        return c

    pltpu.make_async_copy(send1.at[slot_me], recv1.at[me], r1).start()
    lax.fori_loop(1, DEVICES, start1, 0)

    def turn(s, c):
        blk = pup[:, pl.ds(pl.multiple_of(s * LANES, LANES), LANES)].T
        other = swap(blk)
        half = lane_id(LANES) < 64
        tmp_r[...] = jnp.where(half, blk, other)
        tmp_i[...] = jnp.where(half, other, blk) * sgn
        for v in range(4):
            pup_r[v * 32 : (v + 1) * 32, s, :] = tmp_r[pl.ds(v, 32, stride=4), :]
            pup_i[v * 32 : (v + 1) * 32, s, :] = tmp_i[pl.ds(v, 32, stride=4), :]
        return c

    lax.fori_loop(0, STRIPS, turn, 0)

    src = lax.broadcasted_iota(jnp.int32, (Q, Q), 0)
    dst = lax.broadcasted_iota(jnp.int32, (Q, Q), 1)
    perm[...] = jnp.where(src == 4 * (dst & 127) + (dst >> 7), 1.0, 0.0).astype(BF16)
    for g in range(4):
        root = jnp.sqrt(meas[:, g * Q : (g + 1) * Q])
        high = root.astype(BF16)
        low = (root - high.astype(F32)).astype(BF16)
        moved = jnp.dot(high, perm[...], preferred_element_type=F32) + jnp.dot(low, perm[...], preferred_element_type=F32)
        for q in range(4):
            smq[q, :, g * LANES : (g + 1) * LANES] = moved[:, q * LANES : (q + 1) * LANES]

    fetch[0].wait()
    pltpu.make_async_copy(recv1, recv1, r1).wait()

    def shift(e):
        return off[led * PER + e, 0] & 127

    def send_plane(src, dst, ssem, rsem):
        pltpu.make_async_copy(src.at[pl.ds(pl.multiple_of(block * 64, 64), 64)], dst.at[block], rsem).start()

        def go(i, c):
            b = (block + i) & 31
            pltpu.make_async_remote_copy(
                src_ref=src.at[pl.ds(pl.multiple_of(b * 64, 64), 64)],
                dst_ref=dst.at[block],
                send_sem=ssem,
                recv_sem=rsem,
                device_id=plane(b),
                device_id_type=MESH,
            ).start()
            return c

        lax.fori_loop(1, BLOCKS, go, 0)

    for e in range(PER):
        delta = shift(e)

        def product(w, c):
            d = 4 * (w & 31) + (w >> 5)
            win = recv1[(d + delta) & 127, e].astype(F32)
            prod = win * pup_r[w] + swap(win) * pup_i[w]
            at = pl.multiple_of((w & 31) * STRIPS, STRIPS)
            x1[w >> 5, pl.ds(at, STRIPS), :] = prod.astype(BF16)
            x1[w >> 5, pl.ds(at + Q, STRIPS), :] = (swap(prod) * sgn).astype(BF16)
            return c

        lax.fori_loop(0, DEVICES, product, 0, unroll=8)

        def first(v, c):
            ys[v] = jnp.dot(t1[v], x1[v], preferred_element_type=F32)
            return c

        lax.fori_loop(0, 4, first, 0)

        def butterfly(i, c):
            at = pl.multiple_of(i * 64, 64)
            rows = pl.ds(at, 64)
            y0, y1, y2, y3 = (ys[v, rows, :] for v in range(4))
            even, odd = y0 + y2, y1 + y3
            diff, turned = y0 - y2, swap(y1 - y3) * sgn
            for u, value in enumerate((even + odd, diff + turned, even - odd, diff - turned)):
                send2[e, pl.ds(at + u * Q, 64), :] = value.astype(BF16)
            return c

        lax.fori_loop(0, 8, butterfly, 0)
        send_plane(send2.at[e], recv2.at[e], s2.at[e], r2.at[e])

    fetch[1].wait()
    fetch[2].wait()
    for e in range(PER):
        pltpu.make_async_copy(recv2.at[e], recv2.at[e], r2.at[e]).wait()
        for b in range(8):
            a0, a1, a2, a3 = (recv2[e, b + 8 * u].astype(F32) for u in range(4))
            even, odd = a0 + a2, a1 + a3
            diff, turned = a0 - a2, swap(a1 - a3) * sgn
            for q, value in enumerate((even + odd, diff + turned, even - odd, diff - turned)):
                xq[q, :, b * LANES : (b + 1) * LANES] = value.astype(BF16)

        def field(q, c):
            got = jnp.dot(xq[q], t2[q], preferred_element_type=F32)
            re, im = got[:, :Q], got[:, Q:]
            factor = 1.0 - smq[q, pl.ds(e * 64, 64), :] * lax.rsqrt(jnp.maximum(re * re + im * im, 0.25))
            rq[:, :Q] = (re * factor).astype(BF16)
            rq[:, Q:] = (im * factor).astype(BF16)
            zs[q] = jnp.dot(rq[...], t3[q], preferred_element_type=F32)
            return c

        lax.fori_loop(0, 4, field, 0)
        for b in range(8):
            z0, z1, z2, z3 = (zs[q, :, b * LANES : (b + 1) * LANES] for q in range(4))
            even, odd = z0 + z2, z1 + z3
            diff, turned = z0 - z2, swap(z1 - z3) * sgn
            for u, value in enumerate((even + odd, diff - turned, even - odd, diff + turned)):
                send3[e, (b + 8 * u) * 64 : (b + 8 * u + 1) * 64, :] = value.astype(BF16)
        send_plane(send3.at[e], recv3.at[e], s3.at[e], r3.at[e])

    fetch[3].wait()
    for e in range(PER):
        pltpu.make_async_copy(recv3.at[e], recv3.at[e], r3.at[e]).wait()
        delta = shift(e)

        def fold(i, c):
            at = pl.multiple_of(i * 64, 64)
            a0, a1, a2, a3 = (recv3[e, i + 8 * u].astype(F32) for u in range(4))
            even, odd = a0 + a2, a1 + a3
            diff, turned = a0 - a2, swap(a1 - a3) * sgn
            for q, value in enumerate((even + odd, diff - turned, even - odd, diff + turned)):
                x1[q, pl.ds(at, 64), :] = value.astype(BF16)
                x1[q, pl.ds(at + Q, 64), :] = (swap(value) * (-sgn)).astype(BF16)
            return c

        lax.fori_loop(0, 8, fold, 0)

        def last(q, c):
            got = jnp.dot(t4[q], x1[q], preferred_element_type=F32)
            wg[e, pl.ds(q * 32, 32)] = got.reshape(32, STRIPS, LANES)
            return c

        lax.fori_loop(0, 4, last, 0)

        def pupil_sum(w, c):
            rows = pl.ds(pl.multiple_of(w * STRIPS, STRIPS), STRIPS)
            d = 4 * (w & 31) + (w >> 5)
            win = recv1[(d + delta) & 127, e].astype(F32)
            grad = wg[e, w]
            other = swap(win)
            half = lane_id(STRIPS) < 64
            value = grad * jnp.where(half, win, other) - swap(grad) * (jnp.where(half, other, win) * sgn)
            if e == 0:
                pg[rows, :] = value
            else:
                value = value + pg[rows, :]
                pg[rows, :] = value
                pg16[w >> 5, pl.ds(pl.multiple_of((w & 31) * STRIPS, STRIPS), STRIPS), :] = value.astype(BF16)
            return c

        lax.fori_loop(0, DEVICES, pupil_sum, 0, unroll=8)

        def term(d, c):
            w0 = (d - delta) & 127
            w = (w0 & 3) * 32 + (w0 >> 2)
            grad = wg[e, w]
            send4[d, e] = (grad * pup_r[w] - swap(grad) * pup_i[w]).astype(BF16)
            return c

        lax.fori_loop(0, DEVICES, term, 0, unroll=8)

    def along(i):
        return {"band": band, "led": (led + i) & 3, "pencil": pencil}

    for i in range(1, GROUPS):
        pltpu.make_async_remote_copy(
            src_ref=pg16.at[(led + i) & 3], dst_ref=rsr.at[led], send_sem=s5.at[i - 1], recv_sem=r5,
            device_id=along(i), device_id_type=MESH,
        ).start()

    def start4(i, c):
        d = (me + i) & 127
        pltpu.make_async_remote_copy(
            src_ref=send4.at[d], dst_ref=recv4.at[slot_me], send_sem=s4, recv_sem=r4, device_id=device(d), device_id_type=MESH
        ).start()
        return c

    pltpu.make_async_copy(send4.at[me], recv4.at[slot_me], r4).start()
    lax.fori_loop(1, DEVICES, start4, 0)

    pltpu.make_async_copy(rsr.at[pl.ds(0, 3)], rsr.at[pl.ds(0, 3)], r5).wait()
    total = pg[pl.ds(pl.multiple_of(led * Q, Q), Q), :]
    for i in range(1, GROUPS):
        total = total + rsr[(led + i) & 3].astype(F32)
    agr[led] = total.astype(BF16)
    for i in range(1, GROUPS):
        pltpu.make_async_remote_copy(
            src_ref=agr.at[led], dst_ref=agr.at[led], send_sem=s6.at[i - 1], recv_sem=r6,
            device_id=along(i), device_id_type=MESH,
        ).start()
    pltpu.make_async_copy(agr.at[pl.ds(0, 3)], agr.at[pl.ds(0, 3)], r6).wait()

    for v in range(4):
        pg[v * Q : (v + 1) * Q, :] = agr[v].astype(F32)

    def back(s, c):
        for v in range(4):
            tmp_r[pl.ds(v, 32, stride=4), :] = pg[pl.ds(v * Q + s, 32, stride=STRIPS), :]
        pgout[:, pl.ds(pl.multiple_of(s * LANES, LANES), LANES)] = tmp_r[...].T
        return c

    lax.fori_loop(0, STRIPS, back, 0)

    pltpu.make_async_copy(send1.at[pl.ds(0, 127)], send1.at[pl.ds(0, 127)], s1).wait()
    for e in range(PER):
        part = pl.ds(0, W - 64)
        pltpu.make_async_copy(send2.at[e, part], send2.at[e, part], s2.at[e]).wait()
        pltpu.make_async_copy(send3.at[e, part], send3.at[e, part], s3.at[e]).wait()
    for i in range(1, GROUPS):
        pltpu.make_async_copy(pg16.at[0], pg16.at[0], s5.at[i - 1]).wait()
        pltpu.make_async_copy(agr.at[0], agr.at[0], s6.at[i - 1]).wait()
    pltpu.make_async_copy(send4.at[pl.ds(0, 127)], send4.at[pl.ds(0, 127)], s4).wait()
    pltpu.make_async_copy(recv4, recv4, r4).wait()


VMEM = pl.BlockSpec(memory_space=pltpu.VMEM)
SMEM = pl.BlockSpec(memory_space=pltpu.SMEM)
ANY = pl.BlockSpec(memory_space=pl.ANY)
EXCHANGE = (DEVICES, PER, STRIPS, LANES)


def local(spectrum, pupil, measured, offsets):
    small = pltpu.CompilerParams(vmem_limit_bytes=24 << 20)
    rows = spectrum.shape[1]
    tiles = spectrum.shape[3] // LANES
    x = spectrum.reshape(rows, 2, tiles, LANES).transpose(0, 2, 1, 3).reshape(rows * tiles * 2, LANES)
    send1 = pl.pallas_call(
        cut_kernel, out_shape=jax.ShapeDtypeStruct(EXCHANGE, BF16), in_specs=[SMEM, VMEM], out_specs=VMEM,
        compiler_params=small, name="cut",
    )(offsets, x)
    pup = pupil.transpose(0, 2, 1).reshape(LANES, W)
    meas = measured.reshape(PER * 64, W)
    dma = pltpu.SemaphoreType.DMA
    recv4, pgrad = pl.pallas_call(
        core_kernel,
        out_shape=(jax.ShapeDtypeStruct(EXCHANGE, BF16), jax.ShapeDtypeStruct((LANES, W), F32)),
        in_specs=[SMEM, VMEM, VMEM, VMEM, ANY, ANY, ANY, ANY],
        out_specs=(VMEM, VMEM),
        scratch_shapes=[
            pltpu.VMEM((4, Q, 2 * Q), BF16),
            pltpu.VMEM((4, 2 * Q, 2 * Q), BF16),
            pltpu.VMEM((4, 2 * Q, 2 * Q), BF16),
            pltpu.VMEM((4, Q, 2 * Q), BF16),
            pltpu.VMEM(EXCHANGE, BF16),
            pltpu.VMEM((DEVICES, STRIPS, LANES), F32),
            pltpu.VMEM((DEVICES, STRIPS, LANES), F32),
            pltpu.VMEM((LANES, LANES), F32),
            pltpu.VMEM((LANES, LANES), F32),
            pltpu.VMEM((Q, Q), BF16),
            pltpu.VMEM((4, PER * 64, Q), F32),
            pltpu.VMEM((4, 2 * Q, LANES), BF16),
            pltpu.VMEM((4, Q, LANES), F32),
            pltpu.VMEM((PER, W, LANES), BF16),
            pltpu.VMEM((PER, BLOCKS, 64, LANES), BF16),
            pltpu.VMEM((4, 64, 2 * Q), BF16),
            pltpu.VMEM((64, 2 * Q), BF16),
            pltpu.VMEM((4, 64, 2 * Q), F32),
            pltpu.VMEM((PER, W, LANES), BF16),
            pltpu.VMEM((PER, BLOCKS, 64, LANES), BF16),
            pltpu.VMEM((PER, DEVICES, STRIPS, LANES), F32),
            pltpu.VMEM(EXCHANGE, BF16),
            pltpu.VMEM((W, LANES), F32),
            pltpu.VMEM((4, Q, LANES), BF16),
            pltpu.VMEM((4, Q, LANES), BF16),
            pltpu.VMEM((4, Q, LANES), BF16),
            dma((4,)), dma, dma, dma((PER,)), dma((PER,)), dma((PER,)), dma((PER,)),
            dma, dma, dma((3,)), dma, dma((3,)), dma,
        ],
        compiler_params=pltpu.CompilerParams(collective_id=0, has_side_effects=True, vmem_limit_bytes=58 << 20),
        name="core",
    )(offsets, send1, pup, meas, *(jnp.asarray(t) for t in tables()))
    total = pl.pallas_call(
        add_kernel, out_shape=jax.ShapeDtypeStruct(x.shape, F32), in_specs=[SMEM, VMEM], out_specs=VMEM,
        compiler_params=small, name="add",
    )(offsets, recv4)
    spec_grad = total.reshape(rows, tiles, 2, LANES).transpose(0, 2, 1, 3).reshape(spectrum.shape)
    return spec_grad, pgrad.reshape(2, 64, W).transpose(0, 2, 1)


def solution(mesh):
    return jax.shard_map(
        local,
        mesh=mesh,
        in_specs=(
            P(("band", "led", "pencil"), None, None, None),
            P(None, None, ("band", "pencil")),
            P("led", ("band", "pencil"), None),
            P(),
        ),
        out_specs=(
            P(("band", "led", "pencil"), None, None, None),
            P(None, None, ("band", "pencil")),
        ),
        check_vma=False,
    )
```

```python
import functools
import math

import jax
import jax.numpy as jnp
import ml_dtypes
import numpy as np
from jax import lax
from jax.experimental import pallas as pl
from jax.experimental.pallas import tpu as pltpu
from jax.sharding import PartitionSpec as P

W = 2048
Q = W // 4
LANES = 128
STRIPS = 16
DEVICES = 128
BLOCKS = 32
GROUPS = 4
PER = 2
LEDS = 8
STEP = 11
MESH = pl.DeviceIdType.MESH
F32 = jnp.float32
BF16 = jnp.bfloat16


def trig(left, right):
    phase = (np.outer(left, right) % W).astype(np.float64) * (2.0 * math.pi / W)
    return np.cos(phase).astype(np.float32), np.sin(phase).astype(np.float32)


@functools.lru_cache(maxsize=None)
def tables():
    low = np.arange(Q)
    rows_fwd, cols_fwd, cols_back, rows_back = [], [], [], []
    for part in range(4):
        j = (4 * np.arange(32)[:, None] + part + LANES * np.arange(STRIPS)[None, :]).reshape(-1)
        c, s = trig(low, j)
        rows_fwd.append(np.concatenate([c, s], axis=1))
        rows_back.append(np.concatenate([c.T, s.T], axis=1) / W)
        n = 4 * low + part
        c, s = trig(low, n)
        c, s = c.reshape(8, 64, Q), s.reshape(8, 64, Q)
        re = np.concatenate([c, s], axis=2)
        im = np.concatenate([-s, c], axis=2)
        both = np.stack([re, im], axis=1).reshape(2 * Q, 2 * Q)
        cols_fwd.append(both / W)
        cols_back.append(both.T)
    return tuple(np.stack(t).astype(ml_dtypes.bfloat16) for t in (rows_fwd, cols_fwd, cols_back, rows_back))


def lane_id(rows):
    return lax.broadcasted_iota(jnp.int32, (rows, LANES), 1)


def swap(x):
    return pltpu.roll(x, 64, 1)


def position():
    return lax.axis_index("band"), lax.axis_index("led"), lax.axis_index("pencil")


def cut_kernel(off, x, out):
    band, led, pencil = position()
    me = band * 16 + led * 4 + pencil
    lane = lane_id(STRIPS)
    half = lane < 64

    def one(l, carry):
        first = (off[0, l] - me + (DEVICES - 1)) >> 7
        col = off[1, l]
        tile, within = col >> 7, col & 127
        keep = lane < LANES - within
        turn = (LANES - within) & 127

        def load(k, part):
            at = first * LANES + 2 * jnp.minimum(tile + k, 63) + part
            return pltpu.roll(x[pl.ds(at, STRIPS, stride=LANES), :], turn, 1)

        re, im = load(0, 0), load(0, 1)
        for k in range(16):
            next_re, next_im = load(k + 1, 0), load(k + 1, 1)
            a = jnp.where(keep, re, next_re)
            b = jnp.where(keep, im, next_im)
            slot = (l >> 1) * BLOCKS + 2 * k
            out[l & 1, slot] = jnp.where(half, a, swap(b)).astype(BF16)
            out[l & 1, slot + 1] = jnp.where(half, swap(a), b).astype(BF16)
            re, im = next_re, next_im
        return carry

    lax.fori_loop(0, LEDS, one, 0)


def add_kernel(off, terms, pgrad, out, pgrad_out):
    band, led, pencil = position()
    me = band * 16 + led * 4 + pencil
    lane = lane_id(STRIPS)
    half = lane < 64

    def clear(i, carry):
        out[pl.ds(pl.multiple_of(i * 256, 256), 256), :] = jnp.zeros((256, LANES), F32)
        return carry

    lax.fori_loop(0, out.shape[0] // 256, clear, 0)
    pgrad_out[...] = pgrad[...]

    def one(l, carry):
        first = (off[0, l] - me + (DEVICES - 1)) >> 7
        col = off[1, l]
        tile, within = col >> 7, col & 127
        low = lane < within

        def place(k, part):
            return pl.ds(first * LANES + 2 * jnp.minimum(tile + k, 63) + part, STRIPS, stride=LANES)

        zero = jnp.zeros((STRIPS, LANES), F32)
        last = (zero, zero)
        values = []
        for k in range(16):
            slot = (l >> 1) * BLOCKS + 2 * k
            a = terms[l & 1, slot].astype(F32)
            b = terms[l & 1, slot + 1].astype(F32)
            now = (
                pltpu.roll(jnp.where(half, a, swap(b)), within, 1),
                pltpu.roll(jnp.where(half, swap(a), b), within, 1),
            )
            values.append([out[place(k, p), :] + jnp.where(low, last[p], now[p]) for p in range(2)])
            last = now
        for k in range(16):
            for p in range(2):
                out[place(k, p), :] = values[k][p]
        for p in range(2):
            out[place(16, p), :] = out[place(16, p), :] + jnp.where(low, last[p], zero)
        return carry

    lax.fori_loop(0, LEDS, one, 0)


def core_kernel(
    off, send1, pup, meas, h1, h2, h3, h4, recv4, pgout,
    t1, t2, t3, t4, recv1_0, recv1_1, pup_r, pup_i, tmp_r, tmp_i, perm, smq, x1, ys, send2, recv2, xq, rq, zs,
    send3, recv3, wg, send4, pg, pg16, rsr, agr,
    tsem, s1, r1, s2, r2, s3, r3, s4, r4, s5, r5, s6, r6,
):
    recv1 = (recv1_0, recv1_1)
    band, led, pencil = position()
    me = band * 16 + led * 4 + pencil
    block = band * 4 + pencil
    slot_me = led * BLOCKS + block
    sgn = jnp.where(lane_id(1) < 64, -1.0, 1.0).astype(F32)

    def device(d):
        return {"band": d >> 4, "led": (d >> 2) & 3, "pencil": d & 3}

    def plane(b):
        return {"band": b >> 2, "led": led, "pencil": b & 3}

    fetch = [pltpu.make_async_copy(h, t, tsem.at[i]) for i, (h, t) in enumerate(((h1, t1), (h2, t2), (h3, t3), (h4, t4)))]
    for f in fetch:
        f.start()

    barrier = pltpu.get_barrier_semaphore()

    def greet(i, c):
        pl.semaphore_signal(barrier, inc=1, device_id=device((me + i) & 127), device_id_type=MESH)
        return c

    lax.fori_loop(1, DEVICES, greet, 0)
    pl.semaphore_wait(barrier, DEVICES - 1)

    for e in range(PER):

        def start1(i, c):
            d = (me + i * STEP) & 127
            slot = ((d >> 2) & 3) * BLOCKS + (d >> 4) * 4 + (d & 3)
            pltpu.make_async_remote_copy(
                src_ref=send1.at[e, slot], dst_ref=recv1[e].at[me], send_sem=s1.at[e], recv_sem=r1.at[e],
                device_id=device(d), device_id_type=MESH,
            ).start()
            return c

        pltpu.make_async_copy(send1.at[e, slot_me], recv1[e].at[me], r1.at[e]).start()
        lax.fori_loop(1, DEVICES, start1, 0)

    def turn(s, c):
        blk = pup[:, pl.ds(pl.multiple_of(s * LANES, LANES), LANES)].T
        other = swap(blk)
        half = lane_id(LANES) < 64
        tmp_r[...] = jnp.where(half, blk, other)
        tmp_i[...] = jnp.where(half, other, blk) * sgn
        for v in range(4):
            pup_r[v * 32 : (v + 1) * 32, s, :] = tmp_r[pl.ds(v, 32, stride=4), :]
            pup_i[v * 32 : (v + 1) * 32, s, :] = tmp_i[pl.ds(v, 32, stride=4), :]
        return c

    lax.fori_loop(0, STRIPS, turn, 0)

    src = lax.broadcasted_iota(jnp.int32, (Q, Q), 0)
    dst = lax.broadcasted_iota(jnp.int32, (Q, Q), 1)
    perm[...] = jnp.where(src == 4 * (dst & 127) + (dst >> 7), 1.0, 0.0).astype(BF16)
    for g in range(4):
        root = jnp.sqrt(meas[:, g * Q : (g + 1) * Q])
        high = root.astype(BF16)
        low = (root - high.astype(F32)).astype(BF16)
        moved = jnp.dot(high, perm[...], preferred_element_type=F32) + jnp.dot(low, perm[...], preferred_element_type=F32)
        for q in range(4):
            smq[q, :, g * LANES : (g + 1) * LANES] = moved[:, q * LANES : (q + 1) * LANES]

    fetch[0].wait()

    def shift(e):
        return off[0, led * PER + e] & 127

    def send_plane(src, dst, ssem, rsem):
        pltpu.make_async_copy(src.at[pl.ds(pl.multiple_of(block * 64, 64), 64)], dst.at[block], rsem).start()

        def go(i, c):
            b = (block + i * STEP) & 31
            pltpu.make_async_remote_copy(
                src_ref=src.at[pl.ds(pl.multiple_of(b * 64, 64), 64)],
                dst_ref=dst.at[block],
                send_sem=ssem,
                recv_sem=rsem,
                device_id=plane(b),
                device_id_type=MESH,
            ).start()
            return c

        lax.fori_loop(1, BLOCKS, go, 0)

    for e in range(PER):
        pltpu.make_async_copy(recv1[e], recv1[e], r1.at[e]).wait()
        delta = shift(e)

        def product(w, c):
            d = 4 * (w & 31) + (w >> 5)
            win = recv1[e][(d + delta) & 127].astype(F32)
            prod = win * pup_r[w] + swap(win) * pup_i[w]
            at = pl.multiple_of((w & 31) * STRIPS, STRIPS)
            x1[w >> 5, pl.ds(at, STRIPS), :] = prod.astype(BF16)
            x1[w >> 5, pl.ds(at + Q, STRIPS), :] = (swap(prod) * sgn).astype(BF16)
            return c

        lax.fori_loop(0, DEVICES, product, 0, unroll=8)

        def first(v, c):
            ys[v] = jnp.dot(t1[v], x1[v], preferred_element_type=F32)
            return c

        lax.fori_loop(0, 4, first, 0)

        def butterfly(i, c):
            at = pl.multiple_of(i * 64, 64)
            rows = pl.ds(at, 64)
            y0, y1, y2, y3 = (ys[v, rows, :] for v in range(4))
            even, odd = y0 + y2, y1 + y3
            diff, turned = y0 - y2, swap(y1 - y3) * sgn
            for u, value in enumerate((even + odd, diff + turned, even - odd, diff - turned)):
                send2[e, pl.ds(at + u * Q, 64), :] = value.astype(BF16)
            return c

        lax.fori_loop(0, 8, butterfly, 0)
        send_plane(send2.at[e], recv2.at[e], s2.at[e], r2.at[e])

    fetch[1].wait()
    fetch[2].wait()
    for e in range(PER):
        pltpu.make_async_copy(recv2.at[e], recv2.at[e], r2.at[e]).wait()
        for b in range(8):
            a0, a1, a2, a3 = (recv2[e, b + 8 * u].astype(F32) for u in range(4))
            even, odd = a0 + a2, a1 + a3
            diff, turned = a0 - a2, swap(a1 - a3) * sgn
            for q, value in enumerate((even + odd, diff + turned, even - odd, diff - turned)):
                xq[q, :, b * LANES : (b + 1) * LANES] = value.astype(BF16)

        def field(q, c):
            got = jnp.dot(xq[q], t2[q], preferred_element_type=F32)
            re, im = got[:, :Q], got[:, Q:]
            factor = 1.0 - smq[q, pl.ds(e * 64, 64), :] * lax.rsqrt(jnp.maximum(re * re + im * im, 0.25))
            rq[:, :Q] = (re * factor).astype(BF16)
            rq[:, Q:] = (im * factor).astype(BF16)
            zs[q] = jnp.dot(rq[...], t3[q], preferred_element_type=F32)
            return c

        lax.fori_loop(0, 4, field, 0)
        for b in range(8):
            z0, z1, z2, z3 = (zs[q, :, b * LANES : (b + 1) * LANES] for q in range(4))
            even, odd = z0 + z2, z1 + z3
            diff, turned = z0 - z2, swap(z1 - z3) * sgn
            for u, value in enumerate((even + odd, diff - turned, even - odd, diff + turned)):
                send3[e, (b + 8 * u) * 64 : (b + 8 * u + 1) * 64, :] = value.astype(BF16)
        send_plane(send3.at[e], recv3.at[e], s3.at[e], r3.at[e])

    fetch[3].wait()
    def along(i):
        return {"band": band, "led": (led + i) & 3, "pencil": pencil}

    for e in range(PER):
        pltpu.make_async_copy(recv3.at[e], recv3.at[e], r3.at[e]).wait()
        delta = shift(e)

        def fold(i, c):
            at = pl.multiple_of(i * 64, 64)
            a0, a1, a2, a3 = (recv3[e, i + 8 * u].astype(F32) for u in range(4))
            even, odd = a0 + a2, a1 + a3
            diff, turned = a0 - a2, swap(a1 - a3) * sgn
            for q, value in enumerate((even + odd, diff - turned, even - odd, diff + turned)):
                x1[q, pl.ds(at, 64), :] = value.astype(BF16)
                x1[q, pl.ds(at + Q, 64), :] = (swap(value) * (-sgn)).astype(BF16)
            return c

        lax.fori_loop(0, 8, fold, 0)

        def last(q, c):
            got = jnp.dot(t4[q], x1[q], preferred_element_type=F32)
            wg[pl.ds(q * 32, 32)] = got.reshape(32, STRIPS, LANES)
            return c

        lax.fori_loop(0, 4, last, 0)

        def pupil_sum(w, c):
            rows = pl.ds(pl.multiple_of(w * STRIPS, STRIPS), STRIPS)
            d = 4 * (w & 31) + (w >> 5)
            win = recv1[e][(d + delta) & 127].astype(F32)
            grad = wg[w]
            other = swap(win)
            half = lane_id(STRIPS) < 64
            value = grad * jnp.where(half, win, other) - swap(grad) * (jnp.where(half, other, win) * sgn)
            if e == 0:
                pg[rows, :] = value
            else:
                value = value + pg[rows, :]
                pg[rows, :] = value
                pg16[w >> 5, pl.ds(pl.multiple_of((w & 31) * STRIPS, STRIPS), STRIPS), :] = value.astype(BF16)
            return c

        def term(d, c):
            w0 = (d - delta) & 127
            w = (w0 & 3) * 32 + (w0 >> 2)
            grad = wg[w]
            send4[e, d] = (grad * pup_r[w] - swap(grad) * pup_i[w]).astype(BF16)
            return c

        def start4(i, c):
            d = (me + i * STEP) & 127
            pltpu.make_async_remote_copy(
                src_ref=send4.at[e, d], dst_ref=recv4.at[e, slot_me], send_sem=s4.at[e], recv_sem=r4.at[e],
                device_id=device(d), device_id_type=MESH,
            ).start()
            return c

        if e > 0:
            lax.fori_loop(0, DEVICES, pupil_sum, 0, unroll=8)
            for i in range(1, GROUPS):
                pltpu.make_async_remote_copy(
                    src_ref=pg16.at[(led + i) & 3], dst_ref=rsr.at[led], send_sem=s5.at[i - 1], recv_sem=r5,
                    device_id=along(i), device_id_type=MESH,
                ).start()
        lax.fori_loop(0, DEVICES, term, 0, unroll=8)
        pltpu.make_async_copy(send4.at[e, me], recv4.at[e, slot_me], r4.at[e]).start()
        lax.fori_loop(1, DEVICES, start4, 0)
        if e == 0:
            lax.fori_loop(0, DEVICES, pupil_sum, 0, unroll=8)

    pltpu.make_async_copy(rsr.at[pl.ds(0, 3)], rsr.at[pl.ds(0, 3)], r5).wait()
    total = pg[pl.ds(pl.multiple_of(led * Q, Q), Q), :]
    for i in range(1, GROUPS):
        total = total + rsr[(led + i) & 3].astype(F32)
    agr[led] = total.astype(BF16)
    for i in range(1, GROUPS):
        pltpu.make_async_remote_copy(
            src_ref=agr.at[led], dst_ref=agr.at[led], send_sem=s6.at[i - 1], recv_sem=r6,
            device_id=along(i), device_id_type=MESH,
        ).start()
    pltpu.make_async_copy(agr.at[pl.ds(0, 3)], agr.at[pl.ds(0, 3)], r6).wait()

    for v in range(4):
        pg[v * Q : (v + 1) * Q, :] = agr[v].astype(F32)

    def back(s, c):
        for v in range(4):
            tmp_r[pl.ds(v, 32, stride=4), :] = pg[pl.ds(v * Q + s, 32, stride=STRIPS), :]
        pgout[:, pl.ds(pl.multiple_of(s * LANES, LANES), LANES)] = tmp_r[...].T
        return c

    lax.fori_loop(0, STRIPS, back, 0)

    for e in range(PER):
        part = pl.ds(0, DEVICES - 1)
        pltpu.make_async_copy(send1.at[e, part], send1.at[e, part], s1.at[e]).wait()
        pltpu.make_async_copy(send4.at[e, part], send4.at[e, part], s4.at[e]).wait()
        pltpu.make_async_copy(recv4.at[e], recv4.at[e], r4.at[e]).wait()
        part = pl.ds(0, W - 64)
        pltpu.make_async_copy(send2.at[e, part], send2.at[e, part], s2.at[e]).wait()
        pltpu.make_async_copy(send3.at[e, part], send3.at[e, part], s3.at[e]).wait()
    for i in range(1, GROUPS):
        pltpu.make_async_copy(pg16.at[0], pg16.at[0], s5.at[i - 1]).wait()
        pltpu.make_async_copy(agr.at[0], agr.at[0], s6.at[i - 1]).wait()


VMEM = pl.BlockSpec(memory_space=pltpu.VMEM)
SMEM = pl.BlockSpec(memory_space=pltpu.SMEM)
ANY = pl.BlockSpec(memory_space=pl.ANY)
EXCHANGE = (PER, DEVICES, STRIPS, LANES)


def local(spectrum, pupil, measured, offsets):
    offsets = offsets.T
    small = pltpu.CompilerParams(vmem_limit_bytes=24 << 20)
    rows = spectrum.shape[1]
    tiles = spectrum.shape[3] // LANES
    x = spectrum.reshape(rows, 2, tiles, LANES).transpose(0, 2, 1, 3).reshape(rows * tiles * 2, LANES)
    send1 = pl.pallas_call(
        cut_kernel, out_shape=jax.ShapeDtypeStruct(EXCHANGE, BF16), in_specs=[SMEM, VMEM], out_specs=VMEM,
        compiler_params=small, name="cut",
    )(offsets, x)
    pup = pupil.transpose(0, 2, 1).reshape(LANES, W)
    meas = measured.reshape(PER * 64, W)
    dma = pltpu.SemaphoreType.DMA
    recv4, pgrad = pl.pallas_call(
        core_kernel,
        out_shape=(jax.ShapeDtypeStruct(EXCHANGE, BF16), jax.ShapeDtypeStruct((LANES, W), F32)),
        in_specs=[SMEM, VMEM, VMEM, VMEM, ANY, ANY, ANY, ANY],
        out_specs=(VMEM, VMEM),
        scratch_shapes=[
            pltpu.VMEM((4, Q, 2 * Q), BF16),
            pltpu.VMEM((4, 2 * Q, 2 * Q), BF16),
            pltpu.VMEM((4, 2 * Q, 2 * Q), BF16),
            pltpu.VMEM((4, Q, 2 * Q), BF16),
            pltpu.VMEM(EXCHANGE[1:], BF16),
            pltpu.VMEM(EXCHANGE[1:], BF16),
            pltpu.VMEM((DEVICES, STRIPS, LANES), F32),
            pltpu.VMEM((DEVICES, STRIPS, LANES), F32),
            pltpu.VMEM((LANES, LANES), F32),
            pltpu.VMEM((LANES, LANES), F32),
            pltpu.VMEM((Q, Q), BF16),
            pltpu.VMEM((4, PER * 64, Q), F32),
            pltpu.VMEM((4, 2 * Q, LANES), BF16),
            pltpu.VMEM((4, Q, LANES), F32),
            pltpu.VMEM((PER, W, LANES), BF16),
            pltpu.VMEM((PER, BLOCKS, 64, LANES), BF16),
            pltpu.VMEM((4, 64, 2 * Q), BF16),
            pltpu.VMEM((64, 2 * Q), BF16),
            pltpu.VMEM((4, 64, 2 * Q), F32),
            pltpu.VMEM((PER, W, LANES), BF16),
            pltpu.VMEM((PER, BLOCKS, 64, LANES), BF16),
            pltpu.VMEM((DEVICES, STRIPS, LANES), F32),
            pltpu.VMEM(EXCHANGE, BF16),
            pltpu.VMEM((W, LANES), F32),
            pltpu.VMEM((4, Q, LANES), BF16),
            pltpu.VMEM((4, Q, LANES), BF16),
            pltpu.VMEM((4, Q, LANES), BF16),
            dma((4,)), dma((PER,)), dma((PER,)), dma((PER,)), dma((PER,)), dma((PER,)), dma((PER,)),
            dma((PER,)), dma((PER,)), dma((3,)), dma, dma((3,)), dma,
        ],
        compiler_params=pltpu.CompilerParams(collective_id=0, has_side_effects=True, vmem_limit_bytes=48 << 20),
        name="core",
    )(offsets, send1, pup, meas, *(jnp.asarray(t) for t in tables()))
    total, pgrad = pl.pallas_call(
        add_kernel,
        out_shape=(jax.ShapeDtypeStruct(x.shape, F32), jax.ShapeDtypeStruct((LANES, W), F32)),
        in_specs=[SMEM, VMEM, VMEM],
        out_specs=(VMEM, VMEM),
        compiler_params=small,
        name="add",
    )(offsets, recv4, pgrad)
    spec_grad = total.reshape(rows, tiles, 2, LANES).transpose(0, 2, 1, 3).reshape(spectrum.shape)
    return spec_grad, pgrad.reshape(2, 64, W).transpose(0, 2, 1)


def solution(mesh):
    return jax.shard_map(
        local,
        mesh=mesh,
        in_specs=(
            P(("band", "led", "pencil"), None, None, None),
            P(None, None, ("band", "pencil")),
            P("led", ("band", "pencil"), None),
            P(),
        ),
        out_specs=(
            P(("band", "led", "pencil"), None, None, None),
            P(None, None, ("band", "pencil")),
        ),
        check_vma=False,
    )
```

```python
import functools
import math

import jax
import jax.numpy as jnp
import ml_dtypes
import numpy as np
from jax import lax
from jax.experimental import pallas as pl
from jax.experimental.pallas import tpu as pltpu
from jax.sharding import PartitionSpec as P

W = 2048
Q = W // 4
LANES = 128
STRIPS = 16
DEVICES = 128
BLOCKS = 32
GROUPS = 4
PER = 2
LEDS = 8
SPAN = 40
PAD = 136
STEP = 11
MESH = pl.DeviceIdType.MESH
F32 = jnp.float32
BF16 = jnp.bfloat16


def trig(left, right):
    phase = (np.outer(left, right) % W).astype(np.float64) * (2.0 * math.pi / W)
    return np.cos(phase).astype(np.float32), np.sin(phase).astype(np.float32)


@functools.lru_cache(maxsize=None)
def tables():
    low = np.arange(Q)
    rows_fwd, cols_fwd, cols_back, rows_back = [], [], [], []
    for part in range(4):
        j = (4 * np.arange(32)[:, None] + part + LANES * np.arange(STRIPS)[None, :]).reshape(-1)
        c, s = trig(low, j)
        rows_fwd.append(np.concatenate([c, s], axis=1))
        rows_back.append(np.concatenate([c.T, s.T], axis=1) / W)
        n = 4 * low + part
        c, s = trig(low, n)
        c, s = c.reshape(8, 64, Q), s.reshape(8, 64, Q)
        re = np.concatenate([c, s], axis=2)
        im = np.concatenate([-s, c], axis=2)
        both = np.stack([re, im], axis=1)
        both[1::2] = both[1::2, ::-1]
        both = both.reshape(2 * Q, 2 * Q)
        cols_fwd.append(both / W)
        cols_back.append(both.T)
    return tuple(np.stack(t).astype(ml_dtypes.bfloat16) for t in (rows_fwd, cols_fwd, cols_back, rows_back))


def lane_id(rows):
    return lax.broadcasted_iota(jnp.int32, (rows, LANES), 1)


def swap(x):
    return pltpu.roll(x, 64, 1)


def position():
    return lax.axis_index("band"), lax.axis_index("led"), lax.axis_index("pencil")


def cut_kernel(off, x, out, held, sem):
    band, led, pencil = position()
    me = band * 16 + led * 4 + pencil
    lane = lane_id(STRIPS)
    half = lane < 64

    def start_of(l):
        return pl.multiple_of(jnp.minimum(off[1, l] >> 9, 11) * 8, 8)

    def fetch(l):
        first = (off[0, l] - me + (DEVICES - 1)) >> 7
        source = x.at[pl.ds(first, STRIPS), pl.ds(start_of(l), SPAN)]
        return pltpu.make_async_copy(source, held.at[l], sem.at[l])

    for l in range(LEDS):
        fetch(l).start()

    def one(l, carry):
        col = off[1, l]
        tile, within = col >> 7, col & 127
        keeps = (lane < LANES - within, (lane ^ 64) < LANES - within)
        turns = ((LANES - within) & 127, (LANES + 64 - within) & 127)
        fetch(l).wait()

        def load(k, part):
            return pltpu.roll(held[l, :, 2 * jnp.minimum(tile + k, 63) + part - start_of(l), :], turns[part], 1)

        re, im = load(0, 0), load(0, 1)
        for k in range(16):
            next_re, next_im = load(k + 1, 0), load(k + 1, 1)
            a = jnp.where(keeps[0], re, next_re)
            b = jnp.where(keeps[1], im, next_im)
            slot = (l >> 1) * BLOCKS + 2 * k
            out[l & 1, slot] = jnp.where(half, a, b).astype(BF16)
            out[l & 1, slot + 1] = jnp.where(half, b, a).astype(BF16)
            re, im = next_re, next_im
        return carry

    lax.fori_loop(0, LEDS, one, 0)


def add_kernel(off, terms, pgrad, out, pgrad_out, acc, sem):
    band, led, pencil = position()
    me = band * 16 + led * 4 + pencil
    lane = lane_id(STRIPS)
    half = lane < 64

    def clear(i, carry):
        acc[i] = jnp.zeros((PAD, LANES), F32)
        return carry

    lax.fori_loop(0, acc.shape[0], clear, 0)
    pgrad_out[...] = pgrad[...]

    def one(l, carry):
        first = (off[0, l] - me + (DEVICES - 1)) >> 7
        col = off[1, l]
        tile, within = col >> 7, col & 127
        low = lane < within

        def place(k, part):
            return pl.ds(first, STRIPS), 2 * (tile + k) + part

        zero = jnp.zeros((STRIPS, LANES), F32)
        last = (zero, zero)
        values = []
        for k in range(16):
            slot = (l >> 1) * BLOCKS + 2 * k
            a = terms[l & 1, slot].astype(F32)
            b = terms[l & 1, slot + 1].astype(F32)
            now = (
                pltpu.roll(jnp.where(half, a, b), within, 1),
                pltpu.roll(jnp.where(half, b, a), within ^ 64, 1),
            )
            for p in range(2):
                rows, at = place(k, p)
                values.append(acc[rows, at, :] + jnp.where(low, last[p], now[p]))
            last = now
        for p in range(2):
            rows, at = place(16, p)
            values.append(acc[rows, at, :] + jnp.where(low, last[p], zero))
        for k in range(17):
            for p in range(2):
                rows, at = place(k, p)
                acc[rows, at, :] = values[2 * k + p]
        return carry

    lax.fori_loop(0, LEDS, one, 0)
    done = pltpu.make_async_copy(acc.at[:, pl.ds(0, LANES)], out, sem)
    done.start()
    done.wait()


def core_kernel(
    off, send1, pup, meas, h1, h2, h3, h4, recv4, pgout,
    t1, t2, t3, t4, recv1_0, recv1_1, pup_r, pup_i, tmp_r, tmp_i, perm, smq, x1, ys, send2, recv2, xq, rq, zs,
    send3, recv3, wg, wo, send4, pg, pg16, rsr, agr,
    tsem, s1, r1, s2, r2, s3, r3, s4, r4, s5, r5, s6, r6,
):
    recv1 = (recv1_0, recv1_1)
    band, led, pencil = position()
    me = band * 16 + led * 4 + pencil
    block = band * 4 + pencil
    slot_me = led * BLOCKS + block
    odd_pencil = pencil & 1

    def sign(odd):
        return jnp.where(((lane_id(1) >> 6) ^ odd) == 0, -1.0, 1.0).astype(F32)

    sgn = sign(odd_pencil)

    def device(d):
        return {"band": d >> 4, "led": (d >> 2) & 3, "pencil": d & 3}

    def plane(b):
        return {"band": b >> 2, "led": led, "pencil": b & 3}

    fetch = [pltpu.make_async_copy(h, t, tsem.at[i]) for i, (h, t) in enumerate(((h1, t1), (h2, t2), (h3, t3), (h4, t4)))]
    for f in fetch:
        f.start()

    barrier = pltpu.get_barrier_semaphore()

    def greet(i, c):
        pl.semaphore_signal(barrier, inc=1, device_id=device((me + i) & 127), device_id_type=MESH)
        return c

    lax.fori_loop(1, DEVICES, greet, 0)
    pl.semaphore_wait(barrier, DEVICES - 1)

    for e in range(PER):

        def start1(i, c):
            d = (me + i * STEP) & 127
            slot = ((d >> 2) & 3) * BLOCKS + (d >> 4) * 4 + (d & 3)
            pltpu.make_async_remote_copy(
                src_ref=send1.at[e, slot], dst_ref=recv1[e].at[me], send_sem=s1.at[e], recv_sem=r1.at[e],
                device_id=device(d), device_id_type=MESH,
            ).start()
            return c

        pltpu.make_async_copy(send1.at[e, slot_me], recv1[e].at[me], r1.at[e]).start()
        lax.fori_loop(1, DEVICES, start1, 0)

    def turn(s, c):
        blk = pup[:, pl.ds(pl.multiple_of(s * LANES, LANES), LANES)].T
        other = swap(blk)
        half = lane_id(LANES) < 64
        tmp_r[...] = jnp.where(half, blk, other)
        tmp_i[...] = jnp.where(half, other, blk) * sgn
        for v in range(4):
            pup_r[v * 32 : (v + 1) * 32, s, :] = tmp_r[pl.ds(v, 32, stride=4), :]
            pup_i[v * 32 : (v + 1) * 32, s, :] = tmp_i[pl.ds(v, 32, stride=4), :]
        return c

    lax.fori_loop(0, STRIPS, turn, 0)

    src = lax.broadcasted_iota(jnp.int32, (Q, Q), 0)
    dst = lax.broadcasted_iota(jnp.int32, (Q, Q), 1)
    perm[...] = jnp.where(src == 4 * (dst & 127) + (dst >> 7), 1.0, 0.0).astype(BF16)
    for g in range(4):
        root = jnp.sqrt(meas[:, g * Q : (g + 1) * Q])
        high = root.astype(BF16)
        low = (root - high.astype(F32)).astype(BF16)
        moved = jnp.dot(high, perm[...], preferred_element_type=F32) + jnp.dot(low, perm[...], preferred_element_type=F32)
        for q in range(4):
            smq[q, :, g * LANES : (g + 1) * LANES] = moved[:, q * LANES : (q + 1) * LANES]

    fetch[0].wait()

    def shift(e):
        return off[0, led * PER + e] & 127

    def send_plane(b, src, dst, ssem, rsem):
        pltpu.make_async_remote_copy(
            src_ref=src.at[pl.ds(pl.multiple_of(b * 64, 64), 64)],
            dst_ref=dst.at[block],
            send_sem=ssem,
            recv_sem=rsem,
            device_id=plane(b),
            device_id_type=MESH,
        ).start()

    def spread(work, src, dst, ssem, rsem):
        def go(i, own):
            at = (3 * i + block) & 7
            work(at)
            for k in range(1 if own else 0, 4):
                send_plane(at + 8 * ((k + (block >> 3)) & 3), src, dst, ssem, rsem)

        def step(i, c):
            go(i, False)
            return c

        lax.fori_loop(1, 8, step, 0)
        go(8, True)
        pltpu.make_async_copy(src.at[pl.ds(pl.multiple_of(block * 64, 64), 64)], dst.at[block], rsem).start()

    for e in range(PER):
        pltpu.make_async_copy(recv1[e], recv1[e], r1.at[e]).wait()
        delta = shift(e)

        def product(g, c):
            d = 32 * (g & 3) + (g >> 2) + delta
            win = jnp.concatenate([recv1[e][(d + 4 * k) & 127] for k in range(8)], axis=0).astype(F32)
            pr = pup_r[pl.ds(8 * g, 8)].reshape(LANES, LANES)
            pi = pup_i[pl.ds(8 * g, 8)].reshape(LANES, LANES)
            other = swap(win)
            at = pl.multiple_of((g & 3) * LANES, LANES)
            x1[g >> 2, pl.ds(at, LANES), :] = (win * pr + other * pi).astype(BF16)
            x1[g >> 2, pl.ds(at + Q, LANES), :] = ((other * pr - win * pi) * sgn).astype(BF16)
            return c

        lax.fori_loop(0, 16, product, 0)

        def first(v, c):
            ys[v] = jnp.dot(t1[v], x1[v], preferred_element_type=F32)
            return c

        lax.fori_loop(0, 4, first, 0)

        def butterfly(i):
            at = pl.multiple_of(i * 64, 64)
            rows = pl.ds(at, 64)
            y0, y1, y2, y3 = (ys[v, rows, :] for v in range(4))
            even, odd = y0 + y2, y1 + y3
            diff, turned = y0 - y2, swap(y1 - y3) * sgn
            for u, value in enumerate((even + odd, diff + turned, even - odd, diff - turned)):
                send2[e, pl.ds(at + u * Q, 64), :] = value.astype(BF16)

        spread(butterfly, send2.at[e], recv2.at[e], s2.at[e], r2.at[e])

    fetch[1].wait()
    fetch[2].wait()
    for e in range(PER):
        pltpu.make_async_copy(recv2.at[e], recv2.at[e], r2.at[e]).wait()
        for b in range(8):
            a0, a1, a2, a3 = (recv2[e, b + 8 * u].astype(F32) for u in range(4))
            even, odd = a0 + a2, a1 + a3
            diff, turned = a0 - a2, swap(a1 - a3) * sign(b & 1)
            for q, value in enumerate((even + odd, diff + turned, even - odd, diff - turned)):
                xq[q, :, b * LANES : (b + 1) * LANES] = value.astype(BF16)

        def field(q, c):
            got = jnp.dot(xq[q], t2[q], preferred_element_type=F32)
            re, im = got[:, :Q], got[:, Q:]
            factor = 1.0 - smq[q, pl.ds(e * 64, 64), :] * lax.rsqrt(jnp.maximum(re * re + im * im, 0.25))
            rq[:, :Q] = (re * factor).astype(BF16)
            rq[:, Q:] = (im * factor).astype(BF16)
            zs[q] = jnp.dot(rq[...], t3[q], preferred_element_type=F32)
            return c

        lax.fori_loop(0, 4, field, 0)
        def combine(i):
            lanes = pl.ds(pl.multiple_of(i * LANES, LANES), LANES)
            z0, z1, z2, z3 = (zs[q, :, lanes] for q in range(4))
            even, odd = z0 + z2, z1 + z3
            diff, turned = z0 - z2, swap(z1 - z3) * sign(i & 1)
            for u, value in enumerate((even + odd, diff - turned, even - odd, diff + turned)):
                send3[e, pl.ds(pl.multiple_of(i * 64, 64) + u * Q, 64), :] = value.astype(BF16)

        spread(combine, send3.at[e], recv3.at[e], s3.at[e], r3.at[e])

    fetch[3].wait()
    def along(i):
        return {"band": band, "led": (led + i) & 3, "pencil": pencil}

    for e in range(PER):
        pltpu.make_async_copy(recv3.at[e], recv3.at[e], r3.at[e]).wait()
        delta = shift(e)

        def fold(i, c):
            at = pl.multiple_of(i * 64, 64)
            a0, a1, a2, a3 = (recv3[e, i + 8 * u].astype(F32) for u in range(4))
            b0, b1, b2, b3 = (swap(a) for a in (a0, a1, a2, a3))
            even, odd, diff, turned = a0 + a2, a1 + a3, a0 - a2, (b1 - b3) * sgn
            back_even, back_odd, back_diff, back_turned = b0 + b2, b1 + b3, b0 - b2, (a1 - a3) * sgn
            for q, (value, other) in enumerate((
                (even + odd, back_even + back_odd),
                (diff - turned, back_diff + back_turned),
                (even - odd, back_even - back_odd),
                (diff + turned, back_diff - back_turned),
            )):
                x1[q, pl.ds(at, 64), :] = value.astype(BF16)
                x1[q, pl.ds(at + Q, 64), :] = (other * (-sgn)).astype(BF16)
            return c

        lax.fori_loop(0, 8, fold, 0)

        def last(q, c):
            got = jnp.dot(t4[q], x1[q], preferred_element_type=F32)
            wg[pl.ds(q * 32, 32)] = got.reshape(32, STRIPS, LANES)
            wo[pl.ds(q * 32, 32)] = swap(got).reshape(32, STRIPS, LANES)
            return c

        lax.fori_loop(0, 4, last, 0)

        def pupil_sum(g, c):
            rows = pl.ds(pl.multiple_of(g * LANES, LANES), LANES)
            d = 32 * (g & 3) + (g >> 2) + delta
            win = jnp.concatenate([recv1[e][(d + 4 * k) & 127] for k in range(8)], axis=0).astype(F32)
            grad = wg[pl.ds(8 * g, 8)].reshape(LANES, LANES)
            other = swap(win)
            real = ((lane_id(LANES) >> 6) ^ odd_pencil) == 0
            turned = wo[pl.ds(8 * g, 8)].reshape(LANES, LANES)
            value = grad * jnp.where(real, win, other) - turned * (jnp.where(real, other, win) * sgn)
            if e == 0:
                pg[rows, :] = value
            else:
                value = value + pg[rows, :]
                pg[rows, :] = value
                pg16[g >> 2, pl.ds(pl.multiple_of((g & 3) * LANES, LANES), LANES), :] = value.astype(BF16)
            return c

        def term(g, own):
            places = [(me + (8 * g + k + 1) * STEP) & 127 for k in range(8)]
            values = []
            for d in places:
                w0 = (d - delta) & 127
                w = (w0 & 3) * 32 + (w0 >> 2)
                values.append((wg[w] * pup_r[w] - wo[w] * pup_i[w]).astype(BF16))
            for d, value in zip(places, values):
                send4[e, d] = value
            for d in places[: 7 if own else 8]:
                pltpu.make_async_remote_copy(
                    src_ref=send4.at[e, d], dst_ref=recv4.at[e, slot_me], send_sem=s4.at[e], recv_sem=r4.at[e],
                    device_id=device(d), device_id_type=MESH,
                ).start()

        def terms(g, c):
            term(g, False)
            return c

        if e > 0:
            lax.fori_loop(0, 16, pupil_sum, 0)
            for i in range(1, GROUPS):
                pltpu.make_async_remote_copy(
                    src_ref=pg16.at[(led + i) & 3], dst_ref=rsr.at[led], send_sem=s5.at[i - 1], recv_sem=r5,
                    device_id=along(i), device_id_type=MESH,
                ).start()
        lax.fori_loop(0, 15, terms, 0)
        term(15, True)
        pltpu.make_async_copy(send4.at[e, me], recv4.at[e, slot_me], r4.at[e]).start()
        if e == 0:
            lax.fori_loop(0, 16, pupil_sum, 0)

    pltpu.make_async_copy(rsr.at[pl.ds(0, 3)], rsr.at[pl.ds(0, 3)], r5).wait()
    total = pg[pl.ds(pl.multiple_of(led * Q, Q), Q), :]
    for i in range(1, GROUPS):
        total = total + rsr[(led + i) & 3].astype(F32)
    agr[led] = total.astype(BF16)
    for i in range(1, GROUPS):
        pltpu.make_async_remote_copy(
            src_ref=agr.at[led], dst_ref=agr.at[led], send_sem=s6.at[i - 1], recv_sem=r6,
            device_id=along(i), device_id_type=MESH,
        ).start()
    pltpu.make_async_copy(agr.at[pl.ds(0, 3)], agr.at[pl.ds(0, 3)], r6).wait()

    for v in range(4):
        pg[v * Q : (v + 1) * Q, :] = agr[v].astype(F32)

    def back(s, c):
        for v in range(4):
            tmp_r[pl.ds(v, 32, stride=4), :] = pg[pl.ds(v * Q + s, 32, stride=STRIPS), :]
        got = tmp_r[...].T
        lanes = pl.ds(pl.multiple_of(s * LANES, LANES), LANES)
        pgout[:64, lanes] = jnp.where(odd_pencil == 0, got[:64], got[64:])
        pgout[64:, lanes] = jnp.where(odd_pencil == 0, got[64:], got[:64])
        return c

    lax.fori_loop(0, STRIPS, back, 0)

    for e in range(PER):
        part = pl.ds(0, DEVICES - 1)
        pltpu.make_async_copy(send1.at[e, part], send1.at[e, part], s1.at[e]).wait()
        pltpu.make_async_copy(send4.at[e, part], send4.at[e, part], s4.at[e]).wait()
        pltpu.make_async_copy(recv4.at[e], recv4.at[e], r4.at[e]).wait()
        part = pl.ds(0, W - 64)
        pltpu.make_async_copy(send2.at[e, part], send2.at[e, part], s2.at[e]).wait()
        pltpu.make_async_copy(send3.at[e, part], send3.at[e, part], s3.at[e]).wait()
    for i in range(1, GROUPS):
        pltpu.make_async_copy(pg16.at[0], pg16.at[0], s5.at[i - 1]).wait()
        pltpu.make_async_copy(agr.at[0], agr.at[0], s6.at[i - 1]).wait()


VMEM = pl.BlockSpec(memory_space=pltpu.VMEM)
SMEM = pl.BlockSpec(memory_space=pltpu.SMEM)
ANY = pl.BlockSpec(memory_space=pl.ANY)
HBM = pl.BlockSpec(memory_space=pltpu.HBM)
EXCHANGE = (PER, DEVICES, STRIPS, LANES)


def local(spectrum, pupil, measured, offsets):
    offsets = offsets.T
    small = pltpu.CompilerParams(vmem_limit_bytes=24 << 20)
    rows = spectrum.shape[1]
    tiles = spectrum.shape[3] // LANES
    dma = pltpu.SemaphoreType.DMA
    x = spectrum.reshape(rows, 2, tiles, LANES).transpose(0, 2, 1, 3).reshape(rows, 2 * tiles, LANES)
    send1 = pl.pallas_call(
        cut_kernel,
        out_shape=jax.ShapeDtypeStruct(EXCHANGE, BF16),
        in_specs=[SMEM, HBM],
        out_specs=VMEM,
        scratch_shapes=[pltpu.VMEM((LEDS, STRIPS, SPAN, LANES), F32), dma((LEDS,))],
        compiler_params=pltpu.CompilerParams(vmem_limit_bytes=60 << 20),
        name="cut",
    )(offsets, x)
    pup = pupil.transpose(0, 2, 1).reshape(LANES, W)
    meas = measured.reshape(PER * 64, W)
    recv4, pgrad = pl.pallas_call(
        core_kernel,
        out_shape=(jax.ShapeDtypeStruct(EXCHANGE, BF16), jax.ShapeDtypeStruct((LANES, W), F32)),
        in_specs=[SMEM, VMEM, VMEM, VMEM, ANY, ANY, ANY, ANY],
        out_specs=(VMEM, VMEM),
        scratch_shapes=[
            pltpu.VMEM((4, Q, 2 * Q), BF16),
            pltpu.VMEM((4, 2 * Q, 2 * Q), BF16),
            pltpu.VMEM((4, 2 * Q, 2 * Q), BF16),
            pltpu.VMEM((4, Q, 2 * Q), BF16),
            pltpu.VMEM(EXCHANGE[1:], BF16),
            pltpu.VMEM(EXCHANGE[1:], BF16),
            pltpu.VMEM((DEVICES, STRIPS, LANES), F32),
            pltpu.VMEM((DEVICES, STRIPS, LANES), F32),
            pltpu.VMEM((LANES, LANES), F32),
            pltpu.VMEM((LANES, LANES), F32),
            pltpu.VMEM((Q, Q), BF16),
            pltpu.VMEM((4, PER * 64, Q), F32),
            pltpu.VMEM((4, 2 * Q, LANES), BF16),
            pltpu.VMEM((4, Q, LANES), F32),
            pltpu.VMEM((PER, W, LANES), BF16),
            pltpu.VMEM((PER, BLOCKS, 64, LANES), BF16),
            pltpu.VMEM((4, 64, 2 * Q), BF16),
            pltpu.VMEM((64, 2 * Q), BF16),
            pltpu.VMEM((4, 64, 2 * Q), F32),
            pltpu.VMEM((PER, W, LANES), BF16),
            pltpu.VMEM((PER, BLOCKS, 64, LANES), BF16),
            pltpu.VMEM((DEVICES, STRIPS, LANES), F32),
            pltpu.VMEM((DEVICES, STRIPS, LANES), F32),
            pltpu.VMEM(EXCHANGE, BF16),
            pltpu.VMEM((W, LANES), F32),
            pltpu.VMEM((4, Q, LANES), BF16),
            pltpu.VMEM((4, Q, LANES), BF16),
            pltpu.VMEM((4, Q, LANES), BF16),
            dma((4,)), dma((PER,)), dma((PER,)), dma((PER,)), dma((PER,)), dma((PER,)), dma((PER,)),
            dma((PER,)), dma((PER,)), dma((3,)), dma, dma((3,)), dma,
        ],
        compiler_params=pltpu.CompilerParams(collective_id=0, has_side_effects=True, vmem_limit_bytes=48 << 20),
        name="core",
    )(offsets, send1, pup, meas, *(jnp.asarray(t) for t in tables()))
    total, pgrad = pl.pallas_call(
        add_kernel,
        out_shape=(jax.ShapeDtypeStruct(x.shape, F32), jax.ShapeDtypeStruct((LANES, W), F32)),
        in_specs=[SMEM, VMEM, VMEM],
        out_specs=(HBM, VMEM),
        scratch_shapes=[pltpu.VMEM((rows, PAD, LANES), F32), dma],
        compiler_params=small,
        name="add",
    )(offsets, recv4, pgrad)
    spec_grad = total.reshape(rows, tiles, 2, LANES).transpose(0, 2, 1, 3).reshape(spectrum.shape)
    return spec_grad, pgrad.reshape(2, 64, W).transpose(0, 2, 1)


def solution(mesh):
    return jax.shard_map(
        local,
        mesh=mesh,
        in_specs=(
            P(("band", "led", "pencil"), None, None, None),
            P(None, None, ("band", "pencil")),
            P("led", ("band", "pencil"), None),
            P(),
        ),
        out_specs=(
            P(("band", "led", "pencil"), None, None, None),
            P(None, None, ("band", "pencil")),
        ),
        check_vma=False,
    )
```

```python
import functools
import math

import jax
import jax.numpy as jnp
import ml_dtypes
import numpy as np
from jax import lax
from jax.experimental import pallas as pl
from jax.experimental.pallas import tpu as pltpu
from jax.sharding import PartitionSpec as P

W = 2048
Q = W // 4
LANES = 128
STRIPS = 16
DEVICES = 128
BLOCKS = 32
GROUPS = 4
PER = 2
LEDS = 8
PAD = 136
STEP = 27
MESH = pl.DeviceIdType.MESH
F32 = jnp.float32
BF16 = jnp.bfloat16


def trig(left, right):
    phase = (np.outer(left, right) % W).astype(np.float64) * (2.0 * math.pi / W)
    return np.cos(phase).astype(np.float32), np.sin(phase).astype(np.float32)


@functools.lru_cache(maxsize=None)
def tables():
    low = np.arange(Q)
    rows_fwd, cols_fwd, cols_back, rows_back = [], [], [], []
    for part in range(4):
        j = (4 * np.arange(32)[:, None] + part + LANES * np.arange(STRIPS)[None, :]).reshape(-1)
        c, s = trig(low, j)
        rows_fwd.append(np.concatenate([c, s], axis=1))
        rows_back.append(np.concatenate([c.T, s.T], axis=1) / W)
        n = 4 * low + part
        c, s = trig(low, n)
        c, s = c.reshape(8, 64, Q), s.reshape(8, 64, Q)
        re = np.concatenate([c, s], axis=2)
        im = np.concatenate([-s, c], axis=2)
        both = np.stack([re, im], axis=1)
        both[1::2] = both[1::2, ::-1]
        both = both.reshape(2 * Q, 2 * Q)
        cols_fwd.append(both / W)
        cols_back.append(both.T)
    return tuple(np.stack(t).astype(ml_dtypes.bfloat16) for t in (rows_fwd, cols_fwd, cols_back, rows_back))


def lane_id(rows):
    return lax.broadcasted_iota(jnp.int32, (rows, LANES), 1)


def swap(x):
    return pltpu.roll(x, 64, 1)


def position():
    return lax.axis_index("band"), lax.axis_index("led"), lax.axis_index("pencil")


def cut_kernel(off, x, out):
    band, led, pencil = position()
    me = band * 16 + led * 4 + pencil
    lane = lane_id(STRIPS)
    half = lane < 64

    def one(l, carry):
        first = (off[0, l] - me + (DEVICES - 1)) >> 7
        col = off[1, l]
        tile, within = col >> 7, col & 127
        keeps = (lane < LANES - within, (lane ^ 64) < LANES - within)
        turns = ((LANES - within) & 127, (LANES + 64 - within) & 127)

        def load(k, part):
            return pltpu.roll(x[pl.ds(first, STRIPS), 2 * jnp.minimum(tile + k, 63) + part, :], turns[part], 1)

        re, im = load(0, 0), load(0, 1)
        for k in range(16):
            next_re, next_im = load(k + 1, 0), load(k + 1, 1)
            a = jnp.where(keeps[0], re, next_re)
            b = jnp.where(keeps[1], im, next_im)
            slot = (l >> 1) * BLOCKS + 2 * k
            out[l & 1, slot] = jnp.where(half, a, b).astype(BF16)
            out[l & 1, slot + 1] = jnp.where(half, b, a).astype(BF16)
            re, im = next_re, next_im
        return carry

    lax.fori_loop(0, LEDS, one, 0)


def add_kernel(off, terms, pgrad, out, pgrad_out, acc, order, sem):
    band, led, pencil = position()
    me = band * 16 + led * 4 + pencil
    lane = lane_id(STRIPS)
    half = lane < 64

    def clear(i, carry):
        acc[i] = jnp.zeros((PAD, LANES), F32)
        return carry

    lax.fori_loop(0, acc.shape[0], clear, 0)
    pgrad_out[...] = pgrad[...]

    for l in range(LEDS):
        rank = jnp.int32(0)
        for m in range(LEDS):
            if m != l:
                ahead = off[0, m] <= off[0, l] if m < l else off[0, m] < off[0, l]
                rank = rank + ahead.astype(jnp.int32)
        order[rank] = l

    def leave(row, carry):
        pltpu.make_async_copy(acc.at[row, pl.ds(0, LANES)], out.at[row], sem).start()
        return carry

    def one(i, gone):
        l = order[i]
        first = (off[0, l] - me + (DEVICES - 1)) >> 7
        lax.fori_loop(gone, first, leave, 0)
        col = off[1, l]
        tile, within = col >> 7, col & 127
        low = lane < within

        def place(k, part):
            return pl.ds(first, STRIPS), 2 * (tile + k) + part

        zero = jnp.zeros((STRIPS, LANES), F32)
        last = (zero, zero)
        values = []
        for k in range(16):
            slot = (l >> 1) * BLOCKS + 2 * k
            a = terms[l & 1, slot].astype(F32)
            b = terms[l & 1, slot + 1].astype(F32)
            now = (
                pltpu.roll(jnp.where(half, a, b), within, 1),
                pltpu.roll(jnp.where(half, b, a), within ^ 64, 1),
            )
            for p in range(2):
                rows, at = place(k, p)
                values.append(acc[rows, at, :] + jnp.where(low, last[p], now[p]))
            last = now
        for p in range(2):
            rows, at = place(16, p)
            values.append(acc[rows, at, :] + jnp.where(low, last[p], zero))
        for k in range(17):
            for p in range(2):
                rows, at = place(k, p)
                acc[rows, at, :] = values[2 * k + p]
        return first

    gone = lax.fori_loop(0, LEDS, one, jnp.int32(0))
    lax.fori_loop(gone, acc.shape[0], leave, 0)
    pltpu.make_async_copy(acc.at[:, pl.ds(0, LANES)], out, sem).wait()


def core_kernel(
    off, send1, pup, meas, h1, h2, h3, h4, recv4, pgout,
    t1, t2, t3, t4, recv1_0, recv1_1, pup_r, pup_i, tmp_r, tmp_i, perm, smq, x1, ys, send2, recv2, xq, rq, zs,
    send3, recv3, wg, wo, send4, pg, pgn, pg16, rsr, agr,
    tsem, s1, r1, s2, r2, s3, r3, s4, r4, s5, r5, s6, r6,
):
    recv1 = (recv1_0, recv1_1)
    band, led, pencil = position()
    me = band * 16 + led * 4 + pencil
    block = band * 4 + pencil
    slot_me = led * BLOCKS + block
    odd_pencil = pencil & 1

    def sign(odd):
        return jnp.where(((lane_id(1) >> 6) ^ odd) == 0, -1.0, 1.0).astype(F32)

    sgn = sign(odd_pencil)

    def device(d):
        return {"band": d >> 4, "led": (d >> 2) & 3, "pencil": d & 3}

    def plane(b):
        return {"band": b >> 2, "led": led, "pencil": b & 3}

    fetch = [pltpu.make_async_copy(h, t, tsem.at[i]) for i, (h, t) in enumerate(((h1, t1), (h2, t2), (h3, t3), (h4, t4)))]
    for f in fetch:
        f.start()

    barrier = pltpu.get_barrier_semaphore()

    def greet(i, c):
        pl.semaphore_signal(barrier, inc=1, device_id=device((me + i) & 127), device_id_type=MESH)
        return c

    lax.fori_loop(1, DEVICES, greet, 0)
    pl.semaphore_wait(barrier, DEVICES - 1)

    for e in range(PER):

        def start1(i, c):
            d = (me + i * STEP) & 127
            slot = ((d >> 2) & 3) * BLOCKS + (d >> 4) * 4 + (d & 3)
            pltpu.make_async_remote_copy(
                src_ref=send1.at[e, slot], dst_ref=recv1[e].at[me], send_sem=s1.at[e], recv_sem=r1.at[e],
                device_id=device(d), device_id_type=MESH,
            ).start()
            return c

        pltpu.make_async_copy(send1.at[e, slot_me], recv1[e].at[me], r1.at[e]).start()
        lax.fori_loop(1, DEVICES, start1, 0)

    def turn(s, c):
        blk = pup[:, pl.ds(pl.multiple_of(s * LANES, LANES), LANES)].T
        other = swap(blk)
        half = lane_id(LANES) < 64
        tmp_r[...] = jnp.where(half, blk, other)
        tmp_i[...] = jnp.where(half, other, blk) * sgn
        for v in range(4):
            pup_r[v * 32 : (v + 1) * 32, s, :] = tmp_r[pl.ds(v, 32, stride=4), :]
            pup_i[v * 32 : (v + 1) * 32, s, :] = tmp_i[pl.ds(v, 32, stride=4), :]
        return c

    lax.fori_loop(0, STRIPS, turn, 0)

    src = lax.broadcasted_iota(jnp.int32, (Q, Q), 0)
    dst = lax.broadcasted_iota(jnp.int32, (Q, Q), 1)
    perm[...] = jnp.where(src == 4 * (dst & 127) + (dst >> 7), 1.0, 0.0).astype(BF16)
    for g in range(4):
        root = jnp.sqrt(meas[:, g * Q : (g + 1) * Q])
        high = root.astype(BF16)
        low = (root - high.astype(F32)).astype(BF16)
        moved = jnp.dot(high, perm[...], preferred_element_type=F32) + jnp.dot(low, perm[...], preferred_element_type=F32)
        for q in range(4):
            smq[q, :, g * LANES : (g + 1) * LANES] = moved[:, q * LANES : (q + 1) * LANES]

    fetch[0].wait()

    def shift(e):
        return off[0, led * PER + e] & 127

    def send_plane(b, src, dst, ssem, rsem):
        pltpu.make_async_remote_copy(
            src_ref=src.at[pl.ds(pl.multiple_of(b * 64, 64), 64)],
            dst_ref=dst.at[block],
            send_sem=ssem,
            recv_sem=rsem,
            device_id=plane(b),
            device_id_type=MESH,
        ).start()

    def spread(work, src, dst, ssem, rsem):
        def go(i, own):
            at = (5 * i + block) & 7
            work(at)
            for k in range(1 if own else 0, 4):
                send_plane(at + 8 * ((k + (block >> 3)) & 3), src, dst, ssem, rsem)

        def step(i, c):
            go(i, False)
            return c

        lax.fori_loop(1, 8, step, 0)
        go(8, True)
        pltpu.make_async_copy(src.at[pl.ds(pl.multiple_of(block * 64, 64), 64)], dst.at[block], rsem).start()

    for e in range(PER):
        pltpu.make_async_copy(recv1[e], recv1[e], r1.at[e]).wait()
        delta = shift(e)

        def product(g, c):
            d = 32 * (g & 3) + (g >> 2) + delta
            win = jnp.concatenate([recv1[e][(d + 4 * k) & 127] for k in range(8)], axis=0).astype(F32)
            pr = pup_r[pl.ds(8 * g, 8)].reshape(LANES, LANES)
            pi = pup_i[pl.ds(8 * g, 8)].reshape(LANES, LANES)
            other = swap(win)
            at = pl.multiple_of((g & 3) * LANES, LANES)
            x1[g >> 2, pl.ds(at, LANES), :] = (win * pr + other * pi).astype(BF16)
            x1[g >> 2, pl.ds(at + Q, LANES), :] = ((other * pr - win * pi) * sgn).astype(BF16)
            return c

        lax.fori_loop(0, 16, product, 0)

        def first(v, c):
            ys[v] = jnp.dot(t1[v], x1[v], preferred_element_type=F32)
            return c

        lax.fori_loop(0, 4, first, 0)

        def butterfly(i):
            at = pl.multiple_of(i * 64, 64)
            rows = pl.ds(at, 64)
            y0, y1, y2, y3 = (ys[v, rows, :] for v in range(4))
            even, odd = y0 + y2, y1 + y3
            diff, turned = y0 - y2, swap(y1 - y3) * sgn
            for u, value in enumerate((even + odd, diff + turned, even - odd, diff - turned)):
                send2[e, pl.ds(at + u * Q, 64), :] = value.astype(BF16)

        spread(butterfly, send2.at[e], recv2.at[e], s2.at[e], r2.at[e])

    fetch[1].wait()
    fetch[2].wait()
    for e in range(PER):
        pltpu.make_async_copy(recv2.at[e], recv2.at[e], r2.at[e]).wait()
        for b in range(8):
            a0, a1, a2, a3 = (recv2[e, b + 8 * u].astype(F32) for u in range(4))
            even, odd = a0 + a2, a1 + a3
            diff, turned = a0 - a2, swap(a1 - a3) * sign(b & 1)
            for q, value in enumerate((even + odd, diff + turned, even - odd, diff - turned)):
                xq[q, :, b * LANES : (b + 1) * LANES] = value.astype(BF16)

        def field(q, c):
            got = jnp.dot(xq[q], t2[q], preferred_element_type=F32)
            re, im = got[:, :Q], got[:, Q:]
            factor = 1.0 - smq[q, pl.ds(e * 64, 64), :] * lax.rsqrt(jnp.maximum(re * re + im * im, 0.25))
            rq[:, :Q] = (re * factor).astype(BF16)
            rq[:, Q:] = (im * factor).astype(BF16)
            zs[q] = jnp.dot(rq[...], t3[q], preferred_element_type=F32)
            return c

        lax.fori_loop(0, 4, field, 0)
        def combine(i):
            lanes = pl.ds(pl.multiple_of(i * LANES, LANES), LANES)
            z0, z1, z2, z3 = (zs[q, :, lanes] for q in range(4))
            even, odd = z0 + z2, z1 + z3
            diff, turned = z0 - z2, swap(z1 - z3) * sign(i & 1)
            for u, value in enumerate((even + odd, diff - turned, even - odd, diff + turned)):
                send3[e, pl.ds(pl.multiple_of(i * 64, 64) + u * Q, 64), :] = value.astype(BF16)

        spread(combine, send3.at[e], recv3.at[e], s3.at[e], r3.at[e])

    fetch[3].wait()
    def along(i):
        return {"band": band, "led": (led + i) & 3, "pencil": pencil}

    for e in range(PER):
        pltpu.make_async_copy(recv3.at[e], recv3.at[e], r3.at[e]).wait()
        delta = shift(e)

        def fold(i, c):
            at = pl.multiple_of(i * 64, 64)
            a0, a1, a2, a3 = (recv3[e, i + 8 * u].astype(F32) for u in range(4))
            b0, b1, b2, b3 = (swap(a) for a in (a0, a1, a2, a3))
            even, odd, diff, turned = a0 + a2, a1 + a3, a0 - a2, (b1 - b3) * sgn
            back_even, back_odd, back_diff, back_turned = b0 + b2, b1 + b3, b0 - b2, (a1 - a3) * sgn
            for q, (value, other) in enumerate((
                (even + odd, back_even + back_odd),
                (diff - turned, back_diff + back_turned),
                (even - odd, back_even - back_odd),
                (diff + turned, back_diff - back_turned),
            )):
                x1[q, pl.ds(at, 64), :] = value.astype(BF16)
                x1[q, pl.ds(at + Q, 64), :] = (other * (-sgn)).astype(BF16)
            return c

        lax.fori_loop(0, 8, fold, 0)

        def last(q, c):
            got = jnp.dot(t4[q], x1[q], preferred_element_type=F32)
            wg[pl.ds(q * 32, 32)] = got.reshape(32, STRIPS, LANES)
            wo[pl.ds(q * 32, 32)] = swap(got).reshape(32, STRIPS, LANES)
            return c

        lax.fori_loop(0, 4, last, 0)

        def pupil_sum(g, c):
            rows = pl.ds(pl.multiple_of(g * LANES, LANES), LANES)
            d = 32 * (g & 3) + (g >> 2) + delta
            win = jnp.concatenate([recv1[e][(d + 4 * k) & 127] for k in range(8)], axis=0).astype(F32)
            grad = wg[pl.ds(8 * g, 8)].reshape(LANES, LANES)
            other = swap(win)
            real = ((lane_id(LANES) >> 6) ^ odd_pencil) == 0
            turned = wo[pl.ds(8 * g, 8)].reshape(LANES, LANES)
            value = grad * jnp.where(real, win, other) - turned * (jnp.where(real, other, win) * sgn)
            if e == 0:
                pg[rows, :] = value
            else:
                value = (value + pg[rows, :]).reshape(8, STRIPS, LANES)
                for k in range(8):
                    pgn[pl.ds(32 * (g & 3) + 4 * k + (g >> 2), STRIPS, stride=LANES), :] = value[k]
            return c

        def narrow(g, c):
            pg16[g >> 1, pl.ds(pl.multiple_of((g & 1) * 256, 256), 256), :] = pgn[
                pl.ds(pl.multiple_of(g * 256, 256), 256), :
            ].astype(BF16)
            return c

        def term(g, own):
            places = [(me + (8 * g + k + 1) * STEP) & 127 for k in range(8)]
            values = []
            for d in places:
                w0 = (d - delta) & 127
                w = (w0 & 3) * 32 + (w0 >> 2)
                values.append((wg[w] * pup_r[w] - wo[w] * pup_i[w]).astype(BF16))
            for d, value in zip(places, values):
                send4[e, d] = value
            for d in places[: 7 if own else 8]:
                pltpu.make_async_remote_copy(
                    src_ref=send4.at[e, d], dst_ref=recv4.at[e, slot_me], send_sem=s4.at[e], recv_sem=r4.at[e],
                    device_id=device(d), device_id_type=MESH,
                ).start()

        def terms(g, c):
            term(g, False)
            return c

        if e > 0:
            lax.fori_loop(0, 16, pupil_sum, 0)
            lax.fori_loop(0, 8, narrow, 0)
            for i in range(1, GROUPS):
                pltpu.make_async_remote_copy(
                    src_ref=pg16.at[(led + i) & 3], dst_ref=rsr.at[led], send_sem=s5.at[i - 1], recv_sem=r5,
                    device_id=along(i), device_id_type=MESH,
                ).start()
        lax.fori_loop(0, 15, terms, 0)
        term(15, True)
        pltpu.make_async_copy(send4.at[e, me], recv4.at[e, slot_me], r4.at[e]).start()
        if e == 0:
            lax.fori_loop(0, 16, pupil_sum, 0)

    pltpu.make_async_copy(rsr.at[pl.ds(0, 3)], rsr.at[pl.ds(0, 3)], r5).wait()
    for k in range(4):
        total = pgn[pl.ds(pl.multiple_of(led * Q + k * LANES, LANES), LANES), :]
        for i in range(1, GROUPS):
            total = total + rsr[(led + i) & 3, k * LANES : (k + 1) * LANES, :].astype(F32)
        total = total.T
        lanes = slice(k * LANES, (k + 1) * LANES)
        agr[led, :64, lanes] = jnp.where(odd_pencil == 0, total[:64], total[64:]).astype(BF16)
        agr[led, 64:, lanes] = jnp.where(odd_pencil == 0, total[64:], total[:64]).astype(BF16)
    for i in range(1, GROUPS):
        pltpu.make_async_remote_copy(
            src_ref=agr.at[led], dst_ref=agr.at[led], send_sem=s6.at[i - 1], recv_sem=r6,
            device_id=along(i), device_id_type=MESH,
        ).start()
    pltpu.make_async_copy(agr.at[pl.ds(0, 3)], agr.at[pl.ds(0, 3)], r6).wait()

    for v in range(4):
        pgout[:, v * Q : (v + 1) * Q] = agr[v].astype(F32)

    for e in range(PER):
        part = pl.ds(0, DEVICES - 1)
        pltpu.make_async_copy(send1.at[e, part], send1.at[e, part], s1.at[e]).wait()
        pltpu.make_async_copy(send4.at[e, part], send4.at[e, part], s4.at[e]).wait()
        pltpu.make_async_copy(recv4.at[e], recv4.at[e], r4.at[e]).wait()
        part = pl.ds(0, W - 64)
        pltpu.make_async_copy(send2.at[e, part], send2.at[e, part], s2.at[e]).wait()
        pltpu.make_async_copy(send3.at[e, part], send3.at[e, part], s3.at[e]).wait()
    for i in range(1, GROUPS):
        pltpu.make_async_copy(pg16.at[0], pg16.at[0], s5.at[i - 1]).wait()
        pltpu.make_async_copy(agr.at[0], agr.at[0], s6.at[i - 1]).wait()


VMEM = pl.BlockSpec(memory_space=pltpu.VMEM)
SMEM = pl.BlockSpec(memory_space=pltpu.SMEM)
ANY = pl.BlockSpec(memory_space=pl.ANY)
HBM = pl.BlockSpec(memory_space=pltpu.HBM)
EXCHANGE = (PER, DEVICES, STRIPS, LANES)


def local(spectrum, pupil, measured, offsets):
    offsets = offsets.T
    small = pltpu.CompilerParams(vmem_limit_bytes=24 << 20)
    rows = spectrum.shape[1]
    tiles = spectrum.shape[3] // LANES
    dma = pltpu.SemaphoreType.DMA
    x = spectrum.reshape(rows, 2, tiles, LANES).transpose(0, 2, 1, 3).reshape(rows, 2 * tiles, LANES)
    send1 = pl.pallas_call(
        cut_kernel,
        out_shape=jax.ShapeDtypeStruct(EXCHANGE, BF16),
        in_specs=[SMEM, VMEM],
        out_specs=VMEM,
        compiler_params=small,
        name="cut",
    )(offsets, x)
    pup = pupil.transpose(0, 2, 1).reshape(LANES, W)
    meas = measured.reshape(PER * 64, W)
    recv4, pgrad = pl.pallas_call(
        core_kernel,
        out_shape=(jax.ShapeDtypeStruct(EXCHANGE, BF16), jax.ShapeDtypeStruct((LANES, W), F32)),
        in_specs=[SMEM, VMEM, VMEM, VMEM, ANY, ANY, ANY, ANY],
        out_specs=(VMEM, VMEM),
        scratch_shapes=[
            pltpu.VMEM((4, Q, 2 * Q), BF16),
            pltpu.VMEM((4, 2 * Q, 2 * Q), BF16),
            pltpu.VMEM((4, 2 * Q, 2 * Q), BF16),
            pltpu.VMEM((4, Q, 2 * Q), BF16),
            pltpu.VMEM(EXCHANGE[1:], BF16),
            pltpu.VMEM(EXCHANGE[1:], BF16),
            pltpu.VMEM((DEVICES, STRIPS, LANES), F32),
            pltpu.VMEM((DEVICES, STRIPS, LANES), F32),
            pltpu.VMEM((LANES, LANES), F32),
            pltpu.VMEM((LANES, LANES), F32),
            pltpu.VMEM((Q, Q), BF16),
            pltpu.VMEM((4, PER * 64, Q), F32),
            pltpu.VMEM((4, 2 * Q, LANES), BF16),
            pltpu.VMEM((4, Q, LANES), F32),
            pltpu.VMEM((PER, W, LANES), BF16),
            pltpu.VMEM((PER, BLOCKS, 64, LANES), BF16),
            pltpu.VMEM((4, 64, 2 * Q), BF16),
            pltpu.VMEM((64, 2 * Q), BF16),
            pltpu.VMEM((4, 64, 2 * Q), F32),
            pltpu.VMEM((PER, W, LANES), BF16),
            pltpu.VMEM((PER, BLOCKS, 64, LANES), BF16),
            pltpu.VMEM((DEVICES, STRIPS, LANES), F32),
            pltpu.VMEM((DEVICES, STRIPS, LANES), F32),
            pltpu.VMEM(EXCHANGE, BF16),
            pltpu.VMEM((W, LANES), F32),
            pltpu.VMEM((W, LANES), F32),
            pltpu.VMEM((4, Q, LANES), BF16),
            pltpu.VMEM((4, Q, LANES), BF16),
            pltpu.VMEM((4, LANES, Q), BF16),
            dma((4,)), dma((PER,)), dma((PER,)), dma((PER,)), dma((PER,)), dma((PER,)), dma((PER,)),
            dma((PER,)), dma((PER,)), dma((3,)), dma, dma((3,)), dma,
        ],
        compiler_params=pltpu.CompilerParams(collective_id=0, has_side_effects=True, vmem_limit_bytes=48 << 20),
        name="core",
    )(offsets, send1, pup, meas, *(jnp.asarray(t) for t in tables()))
    total, pgrad = pl.pallas_call(
        add_kernel,
        out_shape=(jax.ShapeDtypeStruct(x.shape, F32), jax.ShapeDtypeStruct((LANES, W), F32)),
        in_specs=[SMEM, VMEM, VMEM],
        out_specs=(HBM, VMEM),
        scratch_shapes=[pltpu.VMEM((rows, PAD, LANES), F32), pltpu.SMEM((LEDS,), jnp.int32), dma],
        compiler_params=small,
        name="add",
    )(offsets, recv4, pgrad)
    spec_grad = total.reshape(rows, tiles, 2, LANES).transpose(0, 2, 1, 3).reshape(spectrum.shape)
    return spec_grad, pgrad.reshape(2, 64, W).transpose(0, 2, 1)


def solution(mesh):
    return jax.shard_map(
        local,
        mesh=mesh,
        in_specs=(
            P(("band", "led", "pencil"), None, None, None),
            P(None, None, ("band", "pencil")),
            P("led", ("band", "pencil"), None),
            P(),
        ),
        out_specs=(
            P(("band", "led", "pencil"), None, None, None),
            P(None, None, ("band", "pencil")),
        ),
        check_vma=False,
    )
```

```python
import functools
import math

import jax
import jax.numpy as jnp
import ml_dtypes
import numpy as np
from jax import lax
from jax.experimental import pallas as pl
from jax.experimental.pallas import tpu as pltpu
from jax.sharding import PartitionSpec as P

W = 2048
Q = W // 4
LANES = 128
STRIPS = 16
DEVICES = 128
BLOCKS = 32
GROUPS = 4
PER = 2
LEDS = 8
PAD = 136
STEP = 27
MESH = pl.DeviceIdType.MESH
F32 = jnp.float32
BF16 = jnp.bfloat16


def trig(left, right):
    phase = (np.outer(left, right) % W).astype(np.float64) * (2.0 * math.pi / W)
    return np.cos(phase).astype(np.float32), np.sin(phase).astype(np.float32)


@functools.lru_cache(maxsize=None)
def tables():
    low = np.arange(Q)
    rows_fwd, cols_fwd, cols_back, rows_back = [], [], [], []
    for part in range(4):
        j = (4 * np.arange(32)[:, None] + part + LANES * np.arange(STRIPS)[None, :]).reshape(-1)
        c, s = trig(low, j)
        rows_fwd.append(np.concatenate([c, s], axis=1))
        rows_back.append(np.concatenate([c.T, s.T], axis=1) / W)
        n = 4 * low + part
        c, s = trig(low, n)
        c, s = c.reshape(8, 64, Q), s.reshape(8, 64, Q)
        re = np.concatenate([c, s], axis=2)
        im = np.concatenate([-s, c], axis=2)
        both = np.stack([re, im], axis=1)
        both[1::2] = both[1::2, ::-1]
        both = both.reshape(2 * Q, 2 * Q)
        cols_fwd.append(both / W)
        cols_back.append(both.T)
    return tuple(np.stack(t).astype(ml_dtypes.bfloat16) for t in (rows_fwd, cols_fwd, cols_back, rows_back))


def lane_id(rows):
    return lax.broadcasted_iota(jnp.int32, (rows, LANES), 1)


def swap(x):
    return pltpu.roll(x, 64, 1)


def position():
    return lax.axis_index("band"), lax.axis_index("led"), lax.axis_index("pencil")


def cut_kernel(off, x, out):
    band, led, pencil = position()
    me = band * 16 + led * 4 + pencil
    lane = lane_id(STRIPS)
    half = lane < 64

    def one(l, carry):
        first = (off[0, l] - me + (DEVICES - 1)) >> 7
        col = off[1, l]
        tile, within = col >> 7, col & 127
        keeps = (lane < LANES - within, (lane ^ 64) < LANES - within)
        turns = ((LANES - within) & 127, (LANES + 64 - within) & 127)

        def load(k, part):
            return pltpu.roll(x[pl.ds(first, STRIPS), 2 * jnp.minimum(tile + k, 63) + part, :], turns[part], 1)

        re, im = load(0, 0), load(0, 1)
        for k in range(16):
            next_re, next_im = load(k + 1, 0), load(k + 1, 1)
            a = jnp.where(keeps[0], re, next_re)
            b = jnp.where(keeps[1], im, next_im)
            slot = (l >> 1) * BLOCKS + 2 * k
            out[l & 1, slot] = jnp.where(half, a, b).astype(BF16)
            out[l & 1, slot + 1] = jnp.where(half, b, a).astype(BF16)
            re, im = next_re, next_im
        return carry

    lax.fori_loop(0, LEDS, one, 0)


def add_kernel(off, terms, pgrad, out, pgrad_out, acc, order, sem):
    band, led, pencil = position()
    me = band * 16 + led * 4 + pencil
    lane = lane_id(STRIPS)
    half = lane < 64

    def clear(i, carry):
        acc[i] = jnp.zeros((PAD, LANES), F32)
        return carry

    lax.fori_loop(0, acc.shape[0], clear, 0)
    pgrad_out[...] = pgrad[...]

    for l in range(LEDS):
        rank = jnp.int32(0)
        for m in range(LEDS):
            if m != l:
                ahead = off[0, m] <= off[0, l] if m < l else off[0, m] < off[0, l]
                rank = rank + ahead.astype(jnp.int32)
        order[rank] = l

    def leave(row, carry):
        pltpu.make_async_copy(acc.at[row, pl.ds(0, LANES)], out.at[row], sem).start()
        return carry

    def one(i, gone):
        l = order[i]
        first = (off[0, l] - me + (DEVICES - 1)) >> 7
        lax.fori_loop(gone, first, leave, 0)
        col = off[1, l]
        tile, within = col >> 7, col & 127
        low = lane < within

        def place(k, part):
            return pl.ds(first, STRIPS), 2 * (tile + k) + part

        zero = jnp.zeros((STRIPS, LANES), F32)
        last = (zero, zero)
        values = []
        for k in range(16):
            slot = (l >> 1) * BLOCKS + 2 * k
            a = terms[l & 1, slot].astype(F32)
            b = terms[l & 1, slot + 1].astype(F32)
            now = (
                pltpu.roll(jnp.where(half, a, b), within, 1),
                pltpu.roll(jnp.where(half, b, a), within ^ 64, 1),
            )
            for p in range(2):
                rows, at = place(k, p)
                values.append(acc[rows, at, :] + jnp.where(low, last[p], now[p]))
            last = now
        for p in range(2):
            rows, at = place(16, p)
            values.append(acc[rows, at, :] + jnp.where(low, last[p], zero))
        for k in range(17):
            for p in range(2):
                rows, at = place(k, p)
                acc[rows, at, :] = values[2 * k + p]
        return first

    gone = lax.fori_loop(0, LEDS, one, jnp.int32(0))
    lax.fori_loop(gone, acc.shape[0], leave, 0)
    pltpu.make_async_copy(acc.at[:, pl.ds(0, LANES)], out, sem).wait()


def core_kernel(
    off, send1, pup, meas, h1, h2, h3, h4, recv4, pgout,
    t1, t2, t3, t4, recv1_0, recv1_1, pup_r, pup_i, tmp_r, tmp_i, perm, smq, x1, ys, send2, recv2, xq, rq, zs,
    send3, recv3, wg, wo, send4, pg, pgn, pg16, rsr, agr,
    tsem, s1, r1, s2, r2, s3, r3, s4, r4, s5, r5, s6, r6,
):
    recv1 = (recv1_0, recv1_1)
    band, led, pencil = position()
    me = band * 16 + led * 4 + pencil
    block = band * 4 + pencil
    slot_me = led * BLOCKS + block
    odd_pencil = pencil & 1

    def sign(odd):
        return jnp.where(((lane_id(1) >> 6) ^ odd) == 0, -1.0, 1.0).astype(F32)

    sgn = sign(odd_pencil)

    def device(d):
        return {"band": d >> 4, "led": (d >> 2) & 3, "pencil": d & 3}

    def plane(b):
        return {"band": b >> 2, "led": led, "pencil": b & 3}

    fetch = [pltpu.make_async_copy(h, t, tsem.at[i]) for i, (h, t) in enumerate(((h1, t1), (h2, t2), (h3, t3), (h4, t4)))]
    for f in fetch:
        f.start()

    barrier = pltpu.get_barrier_semaphore()

    def greet(i, c):
        pl.semaphore_signal(barrier, inc=1, device_id=device((me + i) & 127), device_id_type=MESH)
        return c

    lax.fori_loop(1, DEVICES, greet, 0)
    pl.semaphore_wait(barrier, DEVICES - 1)

    for e in range(PER):

        def start1(i, c):
            d = (me + i * STEP) & 127
            slot = ((d >> 2) & 3) * BLOCKS + (d >> 4) * 4 + (d & 3)
            pltpu.make_async_remote_copy(
                src_ref=send1.at[e, slot], dst_ref=recv1[e].at[me], send_sem=s1.at[e], recv_sem=r1.at[e],
                device_id=device(d), device_id_type=MESH,
            ).start()
            return c

        pltpu.make_async_copy(send1.at[e, slot_me], recv1[e].at[me], r1.at[e]).start()
        lax.fori_loop(1, DEVICES, start1, 0)

    def turn(s, c):
        blk = pup[:, pl.ds(pl.multiple_of(s * LANES, LANES), LANES)].T
        other = swap(blk)
        half = lane_id(LANES) < 64
        tmp_r[...] = jnp.where(half, blk, other)
        tmp_i[...] = jnp.where(half, other, blk) * sgn
        for v in range(4):
            pup_r[v * 32 : (v + 1) * 32, s, :] = tmp_r[pl.ds(v, 32, stride=4), :]
            pup_i[v * 32 : (v + 1) * 32, s, :] = tmp_i[pl.ds(v, 32, stride=4), :]
        return c

    lax.fori_loop(0, STRIPS, turn, 0)

    src = lax.broadcasted_iota(jnp.int32, (Q, Q), 0)
    dst = lax.broadcasted_iota(jnp.int32, (Q, Q), 1)
    perm[...] = jnp.where(src == 4 * (dst & 127) + (dst >> 7), 1.0, 0.0).astype(BF16)
    for g in range(4):
        root = jnp.sqrt(meas[:, g * Q : (g + 1) * Q])
        high = root.astype(BF16)
        low = (root - high.astype(F32)).astype(BF16)
        moved = jnp.dot(high, perm[...], preferred_element_type=F32) + jnp.dot(low, perm[...], preferred_element_type=F32)
        for q in range(4):
            smq[q, :, g * LANES : (g + 1) * LANES] = moved[:, q * LANES : (q + 1) * LANES]

    fetch[0].wait()

    def shift(e):
        return off[0, led * PER + e] & 127

    def send_plane(b, src, dst, ssem, rsem):
        pltpu.make_async_remote_copy(
            src_ref=src.at[pl.ds(pl.multiple_of(b * 64, 64), 64)],
            dst_ref=dst.at[block],
            send_sem=ssem,
            recv_sem=rsem,
            device_id=plane(b),
            device_id_type=MESH,
        ).start()

    def spread(work, src, dst, ssem, rsem):
        def go(i, own):
            at = (5 * i + block) & 7
            work(at)
            for k in range(1 if own else 0, 4):
                send_plane(at + 8 * ((k + (block >> 3)) & 3), src, dst, ssem, rsem)

        def step(i, c):
            go(i, False)
            return c

        lax.fori_loop(1, 8, step, 0)
        go(8, True)
        pltpu.make_async_copy(src.at[pl.ds(pl.multiple_of(block * 64, 64), 64)], dst.at[block], rsem).start()

    for e in range(PER):
        pltpu.make_async_copy(recv1[e], recv1[e], r1.at[e]).wait()
        delta = shift(e)

        def product(g, c):
            d = 32 * (g & 3) + (g >> 2) + delta
            win = jnp.concatenate([recv1[e][(d + 4 * k) & 127] for k in range(8)], axis=0).astype(F32)
            pr = pup_r[pl.ds(8 * g, 8)].reshape(LANES, LANES)
            pi = pup_i[pl.ds(8 * g, 8)].reshape(LANES, LANES)
            other = swap(win)
            at = pl.multiple_of((g & 3) * LANES, LANES)
            x1[g >> 2, pl.ds(at, LANES), :] = (win * pr + other * pi).astype(BF16)
            x1[g >> 2, pl.ds(at + Q, LANES), :] = ((other * pr - win * pi) * sgn).astype(BF16)
            return c

        lax.fori_loop(0, 16, product, 0, unroll=2)

        def first(v, c):
            ys[v] = jnp.dot(t1[v], x1[v], preferred_element_type=F32)
            return c

        lax.fori_loop(0, 4, first, 0, unroll=2)

        def butterfly(i):
            at = pl.multiple_of(i * 64, 64)
            rows = pl.ds(at, 64)
            y0, y1, y2, y3 = (ys[v, rows, :] for v in range(4))
            even, odd = y0 + y2, y1 + y3
            diff, turned = y0 - y2, swap(y1 - y3) * sgn
            for u, value in enumerate((even + odd, diff + turned, even - odd, diff - turned)):
                send2[e, pl.ds(at + u * Q, 64), :] = value.astype(BF16)

        spread(butterfly, send2.at[e], recv2.at[e], s2.at[e], r2.at[e])

    fetch[1].wait()
    fetch[2].wait()
    for e in range(PER):
        pltpu.make_async_copy(recv2.at[e], recv2.at[e], r2.at[e]).wait()
        for b in range(8):
            a0, a1, a2, a3 = (recv2[e, b + 8 * u].astype(F32) for u in range(4))
            even, odd = a0 + a2, a1 + a3
            diff, turned = a0 - a2, swap(a1 - a3) * sign(b & 1)
            for q, value in enumerate((even + odd, diff + turned, even - odd, diff - turned)):
                xq[q, :, b * LANES : (b + 1) * LANES] = value.astype(BF16)

        def field(q, c):
            got = jnp.dot(xq[q], t2[q], preferred_element_type=F32)
            re, im = got[:, :Q], got[:, Q:]
            factor = 1.0 - smq[q, pl.ds(e * 64, 64), :] * lax.rsqrt(jnp.maximum(re * re + im * im, 0.25))
            rq[:, :Q] = (re * factor).astype(BF16)
            rq[:, Q:] = (im * factor).astype(BF16)
            zs[q] = jnp.dot(rq[...], t3[q], preferred_element_type=F32)
            return c

        lax.fori_loop(0, 4, field, 0)
        def combine(i):
            lanes = pl.ds(pl.multiple_of(i * LANES, LANES), LANES)
            z0, z1, z2, z3 = (zs[q, :, lanes] for q in range(4))
            even, odd = z0 + z2, z1 + z3
            diff, turned = z0 - z2, swap(z1 - z3) * sign(i & 1)
            for u, value in enumerate((even + odd, diff - turned, even - odd, diff + turned)):
                send3[e, pl.ds(pl.multiple_of(i * 64, 64) + u * Q, 64), :] = value.astype(BF16)

        spread(combine, send3.at[e], recv3.at[e], s3.at[e], r3.at[e])

    fetch[3].wait()
    def along(i):
        return {"band": band, "led": (led + i) & 3, "pencil": pencil}

    for e in range(PER):
        pltpu.make_async_copy(recv3.at[e], recv3.at[e], r3.at[e]).wait()
        delta = shift(e)

        def fold(i, c):
            at = pl.multiple_of(i * 64, 64)
            a0, a1, a2, a3 = (recv3[e, i + 8 * u].astype(F32) for u in range(4))
            b0, b1, b2, b3 = (swap(a) for a in (a0, a1, a2, a3))
            even, odd, diff, turned = a0 + a2, a1 + a3, a0 - a2, (b1 - b3) * sgn
            back_even, back_odd, back_diff, back_turned = b0 + b2, b1 + b3, b0 - b2, (a1 - a3) * sgn
            for q, (value, other) in enumerate((
                (even + odd, back_even + back_odd),
                (diff - turned, back_diff + back_turned),
                (even - odd, back_even - back_odd),
                (diff + turned, back_diff - back_turned),
            )):
                x1[q, pl.ds(at, 64), :] = value.astype(BF16)
                x1[q, pl.ds(at + Q, 64), :] = (other * (-sgn)).astype(BF16)
            return c

        lax.fori_loop(0, 8, fold, 0)

        def last(q, c):
            got = jnp.dot(t4[q], x1[q], preferred_element_type=F32)
            wg[pl.ds(q * 32, 32)] = got.reshape(32, STRIPS, LANES)
            wo[pl.ds(q * 32, 32)] = swap(got).reshape(32, STRIPS, LANES)
            return c

        lax.fori_loop(0, 4, last, 0, unroll=2)

        def pupil_sum(g, c):
            rows = pl.ds(pl.multiple_of(g * LANES, LANES), LANES)
            d = 32 * (g & 3) + (g >> 2) + delta
            win = jnp.concatenate([recv1[e][(d + 4 * k) & 127] for k in range(8)], axis=0).astype(F32)
            grad = wg[pl.ds(8 * g, 8)].reshape(LANES, LANES)
            other = swap(win)
            real = ((lane_id(LANES) >> 6) ^ odd_pencil) == 0
            turned = wo[pl.ds(8 * g, 8)].reshape(LANES, LANES)
            value = grad * jnp.where(real, win, other) - turned * (jnp.where(real, other, win) * sgn)
            if e == 0:
                pg[rows, :] = value
            else:
                value = (value + pg[rows, :]).reshape(8, STRIPS, LANES)
                for k in range(8):
                    pgn[pl.ds(32 * (g & 3) + 4 * k + (g >> 2), STRIPS, stride=LANES), :] = value[k]
            return c

        def narrow(g, c):
            pg16[g >> 1, pl.ds(pl.multiple_of((g & 1) * 256, 256), 256), :] = pgn[
                pl.ds(pl.multiple_of(g * 256, 256), 256), :
            ].astype(BF16)
            return c

        def term(g, own):
            places = [(me + (8 * g + k + 1) * STEP) & 127 for k in range(8)]
            values = []
            for d in places:
                w0 = (d - delta) & 127
                w = (w0 & 3) * 32 + (w0 >> 2)
                values.append((wg[w] * pup_r[w] - wo[w] * pup_i[w]).astype(BF16))
            for d, value in zip(places, values):
                send4[e, d] = value
            for d in places[: 7 if own else 8]:
                pltpu.make_async_remote_copy(
                    src_ref=send4.at[e, d], dst_ref=recv4.at[e, slot_me], send_sem=s4.at[e], recv_sem=r4.at[e],
                    device_id=device(d), device_id_type=MESH,
                ).start()

        def terms(g, c):
            term(g, False)
            return c

        if e > 0:
            lax.fori_loop(0, 16, pupil_sum, 0, unroll=2)
            lax.fori_loop(0, 8, narrow, 0)
            for i in range(1, GROUPS):
                pltpu.make_async_remote_copy(
                    src_ref=pg16.at[(led + i) & 3], dst_ref=rsr.at[led], send_sem=s5.at[i - 1], recv_sem=r5,
                    device_id=along(i), device_id_type=MESH,
                ).start()
        lax.fori_loop(0, 15, terms, 0)
        term(15, True)
        pltpu.make_async_copy(send4.at[e, me], recv4.at[e, slot_me], r4.at[e]).start()
        if e == 0:
            lax.fori_loop(0, 16, pupil_sum, 0, unroll=2)

    pltpu.make_async_copy(rsr.at[pl.ds(0, 3)], rsr.at[pl.ds(0, 3)], r5).wait()
    for k in range(4):
        total = pgn[pl.ds(pl.multiple_of(led * Q + k * LANES, LANES), LANES), :]
        for i in range(1, GROUPS):
            total = total + rsr[(led + i) & 3, k * LANES : (k + 1) * LANES, :].astype(F32)
        total = total.T
        lanes = slice(k * LANES, (k + 1) * LANES)
        agr[led, :64, lanes] = jnp.where(odd_pencil == 0, total[:64], total[64:]).astype(BF16)
        agr[led, 64:, lanes] = jnp.where(odd_pencil == 0, total[64:], total[:64]).astype(BF16)
    for i in range(1, GROUPS):
        pltpu.make_async_remote_copy(
            src_ref=agr.at[led], dst_ref=agr.at[led], send_sem=s6.at[i - 1], recv_sem=r6,
            device_id=along(i), device_id_type=MESH,
        ).start()
    pltpu.make_async_copy(agr.at[pl.ds(0, 3)], agr.at[pl.ds(0, 3)], r6).wait()

    for v in range(4):
        pgout[:, v * Q : (v + 1) * Q] = agr[v].astype(F32)

    for e in range(PER):
        part = pl.ds(0, DEVICES - 1)
        pltpu.make_async_copy(send1.at[e, part], send1.at[e, part], s1.at[e]).wait()
        pltpu.make_async_copy(send4.at[e, part], send4.at[e, part], s4.at[e]).wait()
        pltpu.make_async_copy(recv4.at[e], recv4.at[e], r4.at[e]).wait()
        part = pl.ds(0, W - 64)
        pltpu.make_async_copy(send2.at[e, part], send2.at[e, part], s2.at[e]).wait()
        pltpu.make_async_copy(send3.at[e, part], send3.at[e, part], s3.at[e]).wait()
    for i in range(1, GROUPS):
        pltpu.make_async_copy(pg16.at[0], pg16.at[0], s5.at[i - 1]).wait()
        pltpu.make_async_copy(agr.at[0], agr.at[0], s6.at[i - 1]).wait()


VMEM = pl.BlockSpec(memory_space=pltpu.VMEM)
SMEM = pl.BlockSpec(memory_space=pltpu.SMEM)
ANY = pl.BlockSpec(memory_space=pl.ANY)
HBM = pl.BlockSpec(memory_space=pltpu.HBM)
EXCHANGE = (PER, DEVICES, STRIPS, LANES)


def local(spectrum, pupil, measured, offsets):
    offsets = offsets.T
    small = pltpu.CompilerParams(vmem_limit_bytes=24 << 20)
    rows = spectrum.shape[1]
    tiles = spectrum.shape[3] // LANES
    dma = pltpu.SemaphoreType.DMA
    x = spectrum.reshape(rows, 2, tiles, LANES).transpose(0, 2, 1, 3).reshape(rows, 2 * tiles, LANES)
    send1 = pl.pallas_call(
        cut_kernel,
        out_shape=jax.ShapeDtypeStruct(EXCHANGE, BF16),
        in_specs=[SMEM, VMEM],
        out_specs=VMEM,
        compiler_params=small,
        name="cut",
    )(offsets, x)
    pup = pupil.transpose(0, 2, 1).reshape(LANES, W)
    meas = measured.reshape(PER * 64, W)
    recv4, pgrad = pl.pallas_call(
        core_kernel,
        out_shape=(jax.ShapeDtypeStruct(EXCHANGE, BF16), jax.ShapeDtypeStruct((LANES, W), F32)),
        in_specs=[SMEM, VMEM, VMEM, VMEM, ANY, ANY, ANY, ANY],
        out_specs=(VMEM, VMEM),
        scratch_shapes=[
            pltpu.VMEM((4, Q, 2 * Q), BF16),
            pltpu.VMEM((4, 2 * Q, 2 * Q), BF16),
            pltpu.VMEM((4, 2 * Q, 2 * Q), BF16),
            pltpu.VMEM((4, Q, 2 * Q), BF16),
            pltpu.VMEM(EXCHANGE[1:], BF16),
            pltpu.VMEM(EXCHANGE[1:], BF16),
            pltpu.VMEM((DEVICES, STRIPS, LANES), F32),
            pltpu.VMEM((DEVICES, STRIPS, LANES), F32),
            pltpu.VMEM((LANES, LANES), F32),
            pltpu.VMEM((LANES, LANES), F32),
            pltpu.VMEM((Q, Q), BF16),
            pltpu.VMEM((4, PER * 64, Q), F32),
            pltpu.VMEM((4, 2 * Q, LANES), BF16),
            pltpu.VMEM((4, Q, LANES), F32),
            pltpu.VMEM((PER, W, LANES), BF16),
            pltpu.VMEM((PER, BLOCKS, 64, LANES), BF16),
            pltpu.VMEM((4, 64, 2 * Q), BF16),
            pltpu.VMEM((64, 2 * Q), BF16),
            pltpu.VMEM((4, 64, 2 * Q), F32),
            pltpu.VMEM((PER, W, LANES), BF16),
            pltpu.VMEM((PER, BLOCKS, 64, LANES), BF16),
            pltpu.VMEM((DEVICES, STRIPS, LANES), F32),
            pltpu.VMEM((DEVICES, STRIPS, LANES), F32),
            pltpu.VMEM(EXCHANGE, BF16),
            pltpu.VMEM((W, LANES), F32),
            pltpu.VMEM((W, LANES), F32),
            pltpu.VMEM((4, Q, LANES), BF16),
            pltpu.VMEM((4, Q, LANES), BF16),
            pltpu.VMEM((4, LANES, Q), BF16),
            dma((4,)), dma((PER,)), dma((PER,)), dma((PER,)), dma((PER,)), dma((PER,)), dma((PER,)),
            dma((PER,)), dma((PER,)), dma((3,)), dma, dma((3,)), dma,
        ],
        compiler_params=pltpu.CompilerParams(collective_id=0, has_side_effects=True, vmem_limit_bytes=48 << 20),
        name="core",
    )(offsets, send1, pup, meas, *(jnp.asarray(t) for t in tables()))
    total, pgrad = pl.pallas_call(
        add_kernel,
        out_shape=(jax.ShapeDtypeStruct(x.shape, F32), jax.ShapeDtypeStruct((LANES, W), F32)),
        in_specs=[SMEM, VMEM, VMEM],
        out_specs=(HBM, VMEM),
        scratch_shapes=[pltpu.VMEM((rows, PAD, LANES), F32), pltpu.SMEM((LEDS,), jnp.int32), dma],
        compiler_params=small,
        name="add",
    )(offsets, recv4, pgrad)
    spec_grad = total.reshape(rows, tiles, 2, LANES).transpose(0, 2, 1, 3).reshape(spectrum.shape)
    return spec_grad, pgrad.reshape(2, 64, W).transpose(0, 2, 1)


def solution(mesh):
    return jax.shard_map(
        local,
        mesh=mesh,
        in_specs=(
            P(("band", "led", "pencil"), None, None, None),
            P(None, None, ("band", "pencil")),
            P("led", ("band", "pencil"), None),
            P(),
        ),
        out_specs=(
            P(("band", "led", "pencil"), None, None, None),
            P(None, None, ("band", "pencil")),
        ),
        check_vma=False,
    )
```

```python
import functools
import math

import jax
import jax.numpy as jnp
import ml_dtypes
import numpy as np
from jax import lax
from jax.experimental import pallas as pl
from jax.experimental.pallas import tpu as pltpu
from jax.sharding import PartitionSpec as P

W = 2048
Q = W // 4
LANES = 128
STRIPS = 16
DEVICES = 128
BLOCKS = 32
GROUPS = 4
PER = 2
LEDS = 8
PAD = 136
STEP = 27
MESH = pl.DeviceIdType.MESH
F32 = jnp.float32
BF16 = jnp.bfloat16


def trig(left, right):
    phase = (np.outer(left, right) % W).astype(np.float64) * (2.0 * math.pi / W)
    return np.cos(phase).astype(np.float32), np.sin(phase).astype(np.float32)


@functools.lru_cache(maxsize=None)
def tables():
    low = np.arange(Q)
    rows_fwd, cols_fwd, cols_back, rows_back = [], [], [], []
    for part in range(4):
        j = (4 * np.arange(32)[:, None] + part + LANES * np.arange(STRIPS)[None, :]).reshape(-1)
        c, s = trig(low, j)
        rows_fwd.append(np.concatenate([c, s], axis=1))
        rows_back.append(np.concatenate([c.T, s.T], axis=1) / W)
        n = 4 * low + part
        c, s = trig(low, n)
        c, s = c.reshape(8, 64, Q), s.reshape(8, 64, Q)
        re = np.concatenate([c, s], axis=2)
        im = np.concatenate([-s, c], axis=2)
        both = np.stack([re, im], axis=1)
        both[1::2] = both[1::2, ::-1]
        both = both.reshape(2 * Q, 2 * Q)
        cols_fwd.append(both / W)
        cols_back.append(both.T)
    return tuple(np.stack(t).astype(ml_dtypes.bfloat16) for t in (rows_fwd, cols_fwd, cols_back, rows_back))


def lane_id(rows):
    return lax.broadcasted_iota(jnp.int32, (rows, LANES), 1)


def swap(x):
    return pltpu.roll(x, 64, 1)


def position():
    return lax.axis_index("band"), lax.axis_index("led"), lax.axis_index("pencil")


def cut_kernel(off, x, out):
    band, led, pencil = position()
    me = band * 16 + led * 4 + pencil
    lane = lane_id(STRIPS)
    half = lane < 64

    def one(l, carry):
        first = (off[0, l] - me + (DEVICES - 1)) >> 7
        col = off[1, l]
        tile, within = col >> 7, col & 127
        keeps = (lane < LANES - within, (lane ^ 64) < LANES - within)
        turns = ((LANES - within) & 127, (LANES + 64 - within) & 127)

        def load(k, part):
            return pltpu.roll(x[pl.ds(first, STRIPS), 2 * jnp.minimum(tile + k, 63) + part, :], turns[part], 1)

        re, im = load(0, 0), load(0, 1)
        for k in range(16):
            next_re, next_im = load(k + 1, 0), load(k + 1, 1)
            a = jnp.where(keeps[0], re, next_re)
            b = jnp.where(keeps[1], im, next_im)
            slot = (l >> 1) * BLOCKS + 2 * k
            out[l & 1, slot] = jnp.where(half, a, b).astype(BF16)
            out[l & 1, slot + 1] = jnp.where(half, b, a).astype(BF16)
            re, im = next_re, next_im
        return carry

    lax.fori_loop(0, LEDS, one, 0)


def add_kernel(off, terms, pgrad, out, pgrad_out, acc, order, sem):
    band, led, pencil = position()
    me = band * 16 + led * 4 + pencil
    lane = lane_id(STRIPS)
    half = lane < 64

    def clear(i, carry):
        acc[i] = jnp.zeros((PAD, LANES), F32)
        return carry

    lax.fori_loop(0, acc.shape[0], clear, 0)
    pgrad_out[...] = pgrad[...]

    for l in range(LEDS):
        rank = jnp.int32(0)
        for m in range(LEDS):
            if m != l:
                ahead = off[0, m] <= off[0, l] if m < l else off[0, m] < off[0, l]
                rank = rank + ahead.astype(jnp.int32)
        order[rank] = l

    def leave(row, carry):
        pltpu.make_async_copy(acc.at[row, pl.ds(0, LANES)], out.at[row], sem).start()
        return carry

    def one(i, gone):
        l = order[i]
        first = (off[0, l] - me + (DEVICES - 1)) >> 7
        lax.fori_loop(gone, first, leave, 0)
        col = off[1, l]
        tile, within = col >> 7, col & 127
        low = lane < within

        def place(k, part):
            return pl.ds(first, STRIPS), 2 * (tile + k) + part

        zero = jnp.zeros((STRIPS, LANES), F32)
        last = (zero, zero)
        values = []
        for k in range(16):
            slot = (l >> 1) * BLOCKS + 2 * k
            a = terms[l & 1, slot].astype(F32)
            b = terms[l & 1, slot + 1].astype(F32)
            now = (
                pltpu.roll(jnp.where(half, a, b), within, 1),
                pltpu.roll(jnp.where(half, b, a), within ^ 64, 1),
            )
            for p in range(2):
                rows, at = place(k, p)
                values.append(acc[rows, at, :] + jnp.where(low, last[p], now[p]))
            last = now
        for p in range(2):
            rows, at = place(16, p)
            values.append(acc[rows, at, :] + jnp.where(low, last[p], zero))
        for k in range(17):
            for p in range(2):
                rows, at = place(k, p)
                acc[rows, at, :] = values[2 * k + p]
        return first

    gone = lax.fori_loop(0, LEDS, one, jnp.int32(0))
    lax.fori_loop(gone, acc.shape[0], leave, 0)
    pltpu.make_async_copy(acc.at[:, pl.ds(0, LANES)], out, sem).wait()


def core_kernel(
    off, send1, pup, meas, h1, h2, h3, h4, recv4, pgout,
    t1, t2, t3, t4, recv1_0, recv1_1, pup_r, pup_i, tmp_r, tmp_i, perm, smq, x1, ys, send2, recv2, xq, rq, zs,
    send3, recv3, wg, wo, send4, pg, pgn, pg16, rsr, agr,
    tsem, s1, r1, s2, r2, s3, r3, s4, r4, s5, r5, s6, r6,
):
    recv1 = (recv1_0, recv1_1)
    band, led, pencil = position()
    me = band * 16 + led * 4 + pencil
    block = band * 4 + pencil
    slot_me = led * BLOCKS + block
    odd_pencil = pencil & 1

    def sign(odd):
        return jnp.where(((lane_id(1) >> 6) ^ odd) == 0, -1.0, 1.0).astype(F32)

    sgn = sign(odd_pencil)

    def device(d):
        return {"band": d >> 4, "led": (d >> 2) & 3, "pencil": d & 3}

    def plane(b):
        return {"band": b >> 2, "led": led, "pencil": b & 3}

    fetch = [pltpu.make_async_copy(h, t, tsem.at[i]) for i, (h, t) in enumerate(((h1, t1), (h2, t2), (h3, t3), (h4, t4)))]
    for f in fetch:
        f.start()

    barrier = pltpu.get_barrier_semaphore()

    def greet(i, c):
        pl.semaphore_signal(barrier, inc=1, device_id=device((me + i) & 127), device_id_type=MESH)
        return c

    lax.fori_loop(1, DEVICES, greet, 0)
    pl.semaphore_wait(barrier, DEVICES - 1)

    for e in range(PER):

        def start1(i, c):
            d = (me + i * STEP) & 127
            slot = ((d >> 2) & 3) * BLOCKS + (d >> 4) * 4 + (d & 3)
            pltpu.make_async_remote_copy(
                src_ref=send1.at[e, slot], dst_ref=recv1[e].at[me], send_sem=s1.at[e], recv_sem=r1.at[e],
                device_id=device(d), device_id_type=MESH,
            ).start()
            return c

        pltpu.make_async_copy(send1.at[e, slot_me], recv1[e].at[me], r1.at[e]).start()
        lax.fori_loop(1, DEVICES, start1, 0)

    def turn(s, c):
        blk = pup[:, pl.ds(pl.multiple_of(s * LANES, LANES), LANES)].T
        other = swap(blk)
        half = lane_id(LANES) < 64
        tmp_r[...] = jnp.where(half, blk, other)
        tmp_i[...] = jnp.where(half, other, blk) * sgn
        for v in range(4):
            pup_r[v * 32 : (v + 1) * 32, s, :] = tmp_r[pl.ds(v, 32, stride=4), :]
            pup_i[v * 32 : (v + 1) * 32, s, :] = tmp_i[pl.ds(v, 32, stride=4), :]
        return c

    lax.fori_loop(0, STRIPS, turn, 0)

    src = lax.broadcasted_iota(jnp.int32, (Q, Q), 0)
    dst = lax.broadcasted_iota(jnp.int32, (Q, Q), 1)
    perm[...] = jnp.where(src == 4 * (dst & 127) + (dst >> 7), 1.0, 0.0).astype(BF16)
    for g in range(4):
        root = jnp.sqrt(meas[:, g * Q : (g + 1) * Q])
        high = root.astype(BF16)
        low = (root - high.astype(F32)).astype(BF16)
        moved = jnp.dot(high, perm[...], preferred_element_type=F32) + jnp.dot(low, perm[...], preferred_element_type=F32)
        for q in range(4):
            smq[q, :, g * LANES : (g + 1) * LANES] = moved[:, q * LANES : (q + 1) * LANES]

    fetch[0].wait()

    def shift(e):
        return off[0, led * PER + e] & 127

    def send_plane(b, src, dst, ssem, rsem):
        pltpu.make_async_remote_copy(
            src_ref=src.at[pl.ds(pl.multiple_of(b * 64, 64), 64)],
            dst_ref=dst.at[block],
            send_sem=ssem,
            recv_sem=rsem,
            device_id=plane(b),
            device_id_type=MESH,
        ).start()

    def spread(work, src, dst, ssem, rsem):
        def go(i, own):
            at = (5 * i + block) & 7
            work(at)
            for k in range(1 if own else 0, 4):
                send_plane(at + 8 * ((k + (block >> 3)) & 3), src, dst, ssem, rsem)

        def step(i, c):
            go(i, False)
            return c

        lax.fori_loop(1, 8, step, 0)
        go(8, True)
        pltpu.make_async_copy(src.at[pl.ds(pl.multiple_of(block * 64, 64), 64)], dst.at[block], rsem).start()

    for e in range(PER):
        pltpu.make_async_copy(recv1[e], recv1[e], r1.at[e]).wait()
        delta = shift(e)

        def product(g, c):
            d = 32 * (g & 3) + (g >> 2) + delta
            win = jnp.concatenate([recv1[e][(d + 4 * k) & 127] for k in range(8)], axis=0).astype(F32)
            pr = pup_r[pl.ds(8 * g, 8)].reshape(LANES, LANES)
            pi = pup_i[pl.ds(8 * g, 8)].reshape(LANES, LANES)
            other = swap(win)
            at = pl.multiple_of((g & 3) * LANES, LANES)
            x1[g >> 2, pl.ds(at, LANES), :] = (win * pr + other * pi).astype(BF16)
            x1[g >> 2, pl.ds(at + Q, LANES), :] = ((other * pr - win * pi) * sgn).astype(BF16)
            return c

        lax.fori_loop(0, 16, product, 0, unroll=2)

        def first(v, c):
            ys[v] = jnp.dot(t1[v], x1[v], preferred_element_type=F32)
            return c

        lax.fori_loop(0, 4, first, 0, unroll=4)

        def butterfly(i):
            at = pl.multiple_of(i * 64, 64)
            rows = pl.ds(at, 64)
            y0, y1, y2, y3 = (ys[v, rows, :] for v in range(4))
            even, odd = y0 + y2, y1 + y3
            diff, turned = y0 - y2, swap(y1 - y3) * sgn
            for u, value in enumerate((even + odd, diff + turned, even - odd, diff - turned)):
                send2[e, pl.ds(at + u * Q, 64), :] = value.astype(BF16)

        spread(butterfly, send2.at[e], recv2.at[e], s2.at[e], r2.at[e])

    fetch[1].wait()
    fetch[2].wait()
    for e in range(PER):
        pltpu.make_async_copy(recv2.at[e], recv2.at[e], r2.at[e]).wait()
        for b in range(8):
            a0, a1, a2, a3 = (recv2[e, b + 8 * u].astype(F32) for u in range(4))
            even, odd = a0 + a2, a1 + a3
            diff, turned = a0 - a2, swap(a1 - a3) * sign(b & 1)
            for q, value in enumerate((even + odd, diff + turned, even - odd, diff - turned)):
                xq[q, :, b * LANES : (b + 1) * LANES] = value.astype(BF16)

        def field(q, c):
            got = jnp.dot(xq[q], t2[q], preferred_element_type=F32)
            re, im = got[:, :Q], got[:, Q:]
            factor = 1.0 - smq[q, pl.ds(e * 64, 64), :] * lax.rsqrt(jnp.maximum(re * re + im * im, 0.25))
            rq[q & 1, :, :Q] = (re * factor).astype(BF16)
            rq[q & 1, :, Q:] = (im * factor).astype(BF16)
            zs[q] = jnp.dot(rq[q & 1], t3[q], preferred_element_type=F32)
            return c

        lax.fori_loop(0, 4, field, 0, unroll=2)
        def combine(i):
            lanes = pl.ds(pl.multiple_of(i * LANES, LANES), LANES)
            z0, z1, z2, z3 = (zs[q, :, lanes] for q in range(4))
            even, odd = z0 + z2, z1 + z3
            diff, turned = z0 - z2, swap(z1 - z3) * sign(i & 1)
            for u, value in enumerate((even + odd, diff - turned, even - odd, diff + turned)):
                send3[e, pl.ds(pl.multiple_of(i * 64, 64) + u * Q, 64), :] = value.astype(BF16)

        spread(combine, send3.at[e], recv3.at[e], s3.at[e], r3.at[e])

    fetch[3].wait()
    def along(i):
        return {"band": band, "led": (led + i) & 3, "pencil": pencil}

    for e in range(PER):
        pltpu.make_async_copy(recv3.at[e], recv3.at[e], r3.at[e]).wait()
        delta = shift(e)

        def fold(i, c):
            at = pl.multiple_of(i * 64, 64)
            a0, a1, a2, a3 = (recv3[e, i + 8 * u].astype(F32) for u in range(4))
            b0, b1, b2, b3 = (swap(a) for a in (a0, a1, a2, a3))
            even, odd, diff, turned = a0 + a2, a1 + a3, a0 - a2, (b1 - b3) * sgn
            back_even, back_odd, back_diff, back_turned = b0 + b2, b1 + b3, b0 - b2, (a1 - a3) * sgn
            for q, (value, other) in enumerate((
                (even + odd, back_even + back_odd),
                (diff - turned, back_diff + back_turned),
                (even - odd, back_even - back_odd),
                (diff + turned, back_diff - back_turned),
            )):
                x1[q, pl.ds(at, 64), :] = value.astype(BF16)
                x1[q, pl.ds(at + Q, 64), :] = (other * (-sgn)).astype(BF16)
            return c

        lax.fori_loop(0, 8, fold, 0)

        def last(q, c):
            got = jnp.dot(t4[q], x1[q], preferred_element_type=F32)
            wg[pl.ds(q * 32, 32)] = got.reshape(32, STRIPS, LANES)
            wo[pl.ds(q * 32, 32)] = swap(got).reshape(32, STRIPS, LANES)
            return c

        lax.fori_loop(0, 4, last, 0, unroll=4)

        def pupil_sum(g, c):
            rows = pl.ds(pl.multiple_of(g * LANES, LANES), LANES)
            d = 32 * (g & 3) + (g >> 2) + delta
            win = jnp.concatenate([recv1[e][(d + 4 * k) & 127] for k in range(8)], axis=0).astype(F32)
            grad = wg[pl.ds(8 * g, 8)].reshape(LANES, LANES)
            other = swap(win)
            real = ((lane_id(LANES) >> 6) ^ odd_pencil) == 0
            turned = wo[pl.ds(8 * g, 8)].reshape(LANES, LANES)
            value = grad * jnp.where(real, win, other) - turned * (jnp.where(real, other, win) * sgn)
            if e == 0:
                pg[rows, :] = value
            else:
                value = (value + pg[rows, :]).reshape(8, STRIPS, LANES)
                for k in range(8):
                    pgn[pl.ds(32 * (g & 3) + 4 * k + (g >> 2), STRIPS, stride=LANES), :] = value[k]
            return c

        def narrow(g, c):
            pg16[g >> 1, pl.ds(pl.multiple_of((g & 1) * 256, 256), 256), :] = pgn[
                pl.ds(pl.multiple_of(g * 256, 256), 256), :
            ].astype(BF16)
            return c

        def term(g, own):
            places = [(me + (8 * g + k + 1) * STEP) & 127 for k in range(8)]
            values = []
            for d in places:
                w0 = (d - delta) & 127
                w = (w0 & 3) * 32 + (w0 >> 2)
                values.append((wg[w] * pup_r[w] - wo[w] * pup_i[w]).astype(BF16))
            for d, value in zip(places, values):
                send4[e, d] = value
            for d in places[: 7 if own else 8]:
                pltpu.make_async_remote_copy(
                    src_ref=send4.at[e, d], dst_ref=recv4.at[e, slot_me], send_sem=s4.at[e], recv_sem=r4.at[e],
                    device_id=device(d), device_id_type=MESH,
                ).start()

        def terms(g, c):
            term(g, False)
            return c

        if e > 0:
            lax.fori_loop(0, 16, pupil_sum, 0, unroll=2)
            lax.fori_loop(0, 8, narrow, 0)
            for i in range(1, GROUPS):
                pltpu.make_async_remote_copy(
                    src_ref=pg16.at[(led + i) & 3], dst_ref=rsr.at[led], send_sem=s5.at[i - 1], recv_sem=r5,
                    device_id=along(i), device_id_type=MESH,
                ).start()
        lax.fori_loop(0, 15, terms, 0, unroll=3)
        term(15, True)
        pltpu.make_async_copy(send4.at[e, me], recv4.at[e, slot_me], r4.at[e]).start()
        if e == 0:
            lax.fori_loop(0, 16, pupil_sum, 0, unroll=2)

    pltpu.make_async_copy(rsr.at[pl.ds(0, 3)], rsr.at[pl.ds(0, 3)], r5).wait()
    for k in range(4):
        total = pgn[pl.ds(pl.multiple_of(led * Q + k * LANES, LANES), LANES), :]
        for i in range(1, GROUPS):
            total = total + rsr[(led + i) & 3, k * LANES : (k + 1) * LANES, :].astype(F32)
        total = total.T
        lanes = slice(k * LANES, (k + 1) * LANES)
        agr[led, :64, lanes] = jnp.where(odd_pencil == 0, total[:64], total[64:]).astype(BF16)
        agr[led, 64:, lanes] = jnp.where(odd_pencil == 0, total[64:], total[:64]).astype(BF16)
    for i in range(1, GROUPS):
        pltpu.make_async_remote_copy(
            src_ref=agr.at[led], dst_ref=agr.at[led], send_sem=s6.at[i - 1], recv_sem=r6,
            device_id=along(i), device_id_type=MESH,
        ).start()
    pltpu.make_async_copy(agr.at[pl.ds(0, 3)], agr.at[pl.ds(0, 3)], r6).wait()

    for v in range(4):
        pgout[:, v * Q : (v + 1) * Q] = agr[v].astype(F32)

    for e in range(PER):
        part = pl.ds(0, DEVICES - 1)
        pltpu.make_async_copy(send1.at[e, part], send1.at[e, part], s1.at[e]).wait()
        pltpu.make_async_copy(send4.at[e, part], send4.at[e, part], s4.at[e]).wait()
        pltpu.make_async_copy(recv4.at[e], recv4.at[e], r4.at[e]).wait()
        part = pl.ds(0, W - 64)
        pltpu.make_async_copy(send2.at[e, part], send2.at[e, part], s2.at[e]).wait()
        pltpu.make_async_copy(send3.at[e, part], send3.at[e, part], s3.at[e]).wait()
    for i in range(1, GROUPS):
        pltpu.make_async_copy(pg16.at[0], pg16.at[0], s5.at[i - 1]).wait()
        pltpu.make_async_copy(agr.at[0], agr.at[0], s6.at[i - 1]).wait()


VMEM = pl.BlockSpec(memory_space=pltpu.VMEM)
SMEM = pl.BlockSpec(memory_space=pltpu.SMEM)
ANY = pl.BlockSpec(memory_space=pl.ANY)
HBM = pl.BlockSpec(memory_space=pltpu.HBM)
EXCHANGE = (PER, DEVICES, STRIPS, LANES)


def local(spectrum, pupil, measured, offsets):
    offsets = offsets.T
    small = pltpu.CompilerParams(vmem_limit_bytes=24 << 20)
    rows = spectrum.shape[1]
    tiles = spectrum.shape[3] // LANES
    dma = pltpu.SemaphoreType.DMA
    x = spectrum.reshape(rows, 2, tiles, LANES).transpose(0, 2, 1, 3).reshape(rows, 2 * tiles, LANES)
    send1 = pl.pallas_call(
        cut_kernel,
        out_shape=jax.ShapeDtypeStruct(EXCHANGE, BF16),
        in_specs=[SMEM, VMEM],
        out_specs=VMEM,
        compiler_params=small,
        name="cut",
    )(offsets, x)
    pup = pupil.transpose(0, 2, 1).reshape(LANES, W)
    meas = measured.reshape(PER * 64, W)
    recv4, pgrad = pl.pallas_call(
        core_kernel,
        out_shape=(jax.ShapeDtypeStruct(EXCHANGE, BF16), jax.ShapeDtypeStruct((LANES, W), F32)),
        in_specs=[SMEM, VMEM, VMEM, VMEM, ANY, ANY, ANY, ANY],
        out_specs=(VMEM, VMEM),
        scratch_shapes=[
            pltpu.VMEM((4, Q, 2 * Q), BF16),
            pltpu.VMEM((4, 2 * Q, 2 * Q), BF16),
            pltpu.VMEM((4, 2 * Q, 2 * Q), BF16),
            pltpu.VMEM((4, Q, 2 * Q), BF16),
            pltpu.VMEM(EXCHANGE[1:], BF16),
            pltpu.VMEM(EXCHANGE[1:], BF16),
            pltpu.VMEM((DEVICES, STRIPS, LANES), F32),
            pltpu.VMEM((DEVICES, STRIPS, LANES), F32),
            pltpu.VMEM((LANES, LANES), F32),
            pltpu.VMEM((LANES, LANES), F32),
            pltpu.VMEM((Q, Q), BF16),
            pltpu.VMEM((4, PER * 64, Q), F32),
            pltpu.VMEM((4, 2 * Q, LANES), BF16),
            pltpu.VMEM((4, Q, LANES), F32),
            pltpu.VMEM((PER, W, LANES), BF16),
            pltpu.VMEM((PER, BLOCKS, 64, LANES), BF16),
            pltpu.VMEM((4, 64, 2 * Q), BF16),
            pltpu.VMEM((2, 64, 2 * Q), BF16),
            pltpu.VMEM((4, 64, 2 * Q), F32),
            pltpu.VMEM((PER, W, LANES), BF16),
            pltpu.VMEM((PER, BLOCKS, 64, LANES), BF16),
            pltpu.VMEM((DEVICES, STRIPS, LANES), F32),
            pltpu.VMEM((DEVICES, STRIPS, LANES), F32),
            pltpu.VMEM(EXCHANGE, BF16),
            pltpu.VMEM((W, LANES), F32),
            pltpu.VMEM((W, LANES), F32),
            pltpu.VMEM((4, Q, LANES), BF16),
            pltpu.VMEM((4, Q, LANES), BF16),
            pltpu.VMEM((4, LANES, Q), BF16),
            dma((4,)), dma((PER,)), dma((PER,)), dma((PER,)), dma((PER,)), dma((PER,)), dma((PER,)),
            dma((PER,)), dma((PER,)), dma((3,)), dma, dma((3,)), dma,
        ],
        compiler_params=pltpu.CompilerParams(collective_id=0, has_side_effects=True, vmem_limit_bytes=48 << 20),
        name="core",
    )(offsets, send1, pup, meas, *(jnp.asarray(t) for t in tables()))
    total, pgrad = pl.pallas_call(
        add_kernel,
        out_shape=(jax.ShapeDtypeStruct(x.shape, F32), jax.ShapeDtypeStruct((LANES, W), F32)),
        in_specs=[SMEM, VMEM, VMEM],
        out_specs=(HBM, VMEM),
        scratch_shapes=[pltpu.VMEM((rows, PAD, LANES), F32), pltpu.SMEM((LEDS,), jnp.int32), dma],
        compiler_params=small,
        name="add",
    )(offsets, recv4, pgrad)
    spec_grad = total.reshape(rows, tiles, 2, LANES).transpose(0, 2, 1, 3).reshape(spectrum.shape)
    return spec_grad, pgrad.reshape(2, 64, W).transpose(0, 2, 1)


def solution(mesh):
    return jax.shard_map(
        local,
        mesh=mesh,
        in_specs=(
            P(("band", "led", "pencil"), None, None, None),
            P(None, None, ("band", "pencil")),
            P("led", ("band", "pencil"), None),
            P(),
        ),
        out_specs=(
            P(("band", "led", "pencil"), None, None, None),
            P(None, None, ("band", "pencil")),
        ),
        check_vma=False,
    )
```

```python
import functools
import math

import jax
import jax.numpy as jnp
import ml_dtypes
import numpy as np
from jax import lax
from jax.experimental import pallas as pl
from jax.experimental.pallas import tpu as pltpu
from jax.sharding import PartitionSpec as P

W = 2048
Q = W // 4
LANES = 128
STRIPS = 16
DEVICES = 128
BLOCKS = 32
GROUPS = 4
PER = 2
LEDS = 8
PAD = 136
STEP = 27
MESH = pl.DeviceIdType.MESH
F32 = jnp.float32
BF16 = jnp.bfloat16


def trig(left, right):
    phase = (np.outer(left, right) % W).astype(np.float64) * (2.0 * math.pi / W)
    return np.cos(phase).astype(np.float32), np.sin(phase).astype(np.float32)


@functools.lru_cache(maxsize=None)
def tables():
    low = np.arange(Q)
    rows_fwd, cols_fwd, cols_back, rows_back = [], [], [], []
    for part in range(4):
        j = (4 * np.arange(32)[:, None] + part + LANES * np.arange(STRIPS)[None, :]).reshape(-1)
        c, s = trig(low, j)
        rows_fwd.append(np.concatenate([c, s], axis=1))
        rows_back.append(np.concatenate([c.T, s.T], axis=1) / W)
        n = 4 * low + part
        c, s = trig(low, n)
        c, s = c.reshape(8, 64, Q), s.reshape(8, 64, Q)
        re = np.concatenate([c, s], axis=2)
        im = np.concatenate([-s, c], axis=2)
        both = np.stack([re, im], axis=1)
        both[1::2] = both[1::2, ::-1]
        both = both.reshape(2 * Q, 2 * Q)
        cols_fwd.append(both / W)
        cols_back.append(both.T)
    return tuple(np.stack(t).astype(ml_dtypes.bfloat16) for t in (rows_fwd, cols_fwd, cols_back, rows_back))


def lane_id(rows):
    return lax.broadcasted_iota(jnp.int32, (rows, LANES), 1)


def swap(x):
    return pltpu.roll(x, 64, 1)


def position():
    return lax.axis_index("band"), lax.axis_index("led"), lax.axis_index("pencil")


def cut_kernel(off, x, out):
    band, led, pencil = position()
    me = band * 16 + led * 4 + pencil
    lane = lane_id(STRIPS)
    half = lane < 64

    def one(l, carry):
        first = (off[0, l] - me + (DEVICES - 1)) >> 7
        col = off[1, l]
        tile, within = col >> 7, col & 127
        keeps = (lane < LANES - within, (lane ^ 64) < LANES - within)
        turns = ((LANES - within) & 127, (LANES + 64 - within) & 127)

        def load(k, part):
            return pltpu.roll(x[pl.ds(first, STRIPS), 2 * jnp.minimum(tile + k, 63) + part, :], turns[part], 1)

        re, im = load(0, 0), load(0, 1)
        for k in range(16):
            next_re, next_im = load(k + 1, 0), load(k + 1, 1)
            a = jnp.where(keeps[0], re, next_re)
            b = jnp.where(keeps[1], im, next_im)
            slot = (l >> 1) * BLOCKS + 2 * k
            out[l & 1, slot] = jnp.where(half, a, b).astype(BF16)
            out[l & 1, slot + 1] = jnp.where(half, b, a).astype(BF16)
            re, im = next_re, next_im
        return carry

    lax.fori_loop(0, LEDS, one, 0)


def add_kernel(off, terms, pgrad, out, pgrad_out, acc, order, sem):
    band, led, pencil = position()
    me = band * 16 + led * 4 + pencil
    lane = lane_id(STRIPS)
    half = lane < 64

    def clear(i, carry):
        acc[i] = jnp.zeros((PAD, LANES), F32)
        return carry

    lax.fori_loop(0, acc.shape[0], clear, 0)
    pgrad_out[...] = pgrad[...]

    for l in range(LEDS):
        rank = jnp.int32(0)
        for m in range(LEDS):
            if m != l:
                ahead = off[0, m] <= off[0, l] if m < l else off[0, m] < off[0, l]
                rank = rank + ahead.astype(jnp.int32)
        order[rank] = l

    def leave(row, carry):
        pltpu.make_async_copy(acc.at[row, pl.ds(0, LANES)], out.at[row], sem).start()
        return carry

    def one(i, gone):
        l = order[i]
        first = (off[0, l] - me + (DEVICES - 1)) >> 7
        lax.fori_loop(gone, first, leave, 0)
        col = off[1, l]
        tile, within = col >> 7, col & 127
        low = lane < within

        def place(k, part):
            return pl.ds(first, STRIPS), 2 * (tile + k) + part

        zero = jnp.zeros((STRIPS, LANES), F32)
        last = (zero, zero)
        values = []
        for k in range(16):
            slot = (l >> 1) * BLOCKS + 2 * k
            a = terms[l & 1, slot].astype(F32)
            b = terms[l & 1, slot + 1].astype(F32)
            now = (
                pltpu.roll(jnp.where(half, a, b), within, 1),
                pltpu.roll(jnp.where(half, b, a), within ^ 64, 1),
            )
            for p in range(2):
                rows, at = place(k, p)
                values.append(acc[rows, at, :] + jnp.where(low, last[p], now[p]))
            last = now
        for p in range(2):
            rows, at = place(16, p)
            values.append(acc[rows, at, :] + jnp.where(low, last[p], zero))
        for k in range(17):
            for p in range(2):
                rows, at = place(k, p)
                acc[rows, at, :] = values[2 * k + p]
        return first

    gone = lax.fori_loop(0, LEDS, one, jnp.int32(0))
    lax.fori_loop(gone, acc.shape[0], leave, 0)
    pltpu.make_async_copy(acc.at[:, pl.ds(0, LANES)], out, sem).wait()


def core_kernel(
    off, send1, pup, meas, h1, h2, h3, h4, recv4, pgout,
    t1, t2, t3, t4, recv1_0, recv1_1, pup_r, pup_i, tmp_r, tmp_i, perm, smq, x1, ys, send2, recv2, xq, rq, zs,
    send3, recv3, wg, wo, send4, pg, pgn, pg16, rsr, agr,
    tsem, s1, r1, s2, r2, s3, r3, s4, r4, s5, r5, s6, r6,
):
    recv1 = (recv1_0, recv1_1)
    band, led, pencil = position()
    me = band * 16 + led * 4 + pencil
    block = band * 4 + pencil
    slot_me = led * BLOCKS + block
    odd_pencil = pencil & 1

    def sign(odd):
        return jnp.where(((lane_id(1) >> 6) ^ odd) == 0, -1.0, 1.0).astype(F32)

    sgn = sign(odd_pencil)

    def device(d):
        return {"band": d >> 4, "led": (d >> 2) & 3, "pencil": d & 3}

    def plane(b):
        return {"band": b >> 2, "led": led, "pencil": b & 3}

    fetch = [pltpu.make_async_copy(h, t, tsem.at[i]) for i, (h, t) in enumerate(((h1, t1), (h2, t2), (h3, t3), (h4, t4)))]
    for f in fetch:
        f.start()

    barrier = pltpu.get_barrier_semaphore()

    def greet(i, c):
        pl.semaphore_signal(barrier, inc=1, device_id=device((me + i) & 127), device_id_type=MESH)
        return c

    lax.fori_loop(1, DEVICES, greet, 0)
    pl.semaphore_wait(barrier, DEVICES - 1)

    for e in range(PER):

        def start1(i, c):
            d = (me + i * STEP) & 127
            slot = ((d >> 2) & 3) * BLOCKS + (d >> 4) * 4 + (d & 3)
            pltpu.make_async_remote_copy(
                src_ref=send1.at[e, slot], dst_ref=recv1[e].at[me], send_sem=s1.at[e], recv_sem=r1.at[e],
                device_id=device(d), device_id_type=MESH,
            ).start()
            return c

        pltpu.make_async_copy(send1.at[e, slot_me], recv1[e].at[me], r1.at[e]).start()
        lax.fori_loop(1, DEVICES, start1, 0)

    def turn(s, c):
        blk = pup[:, pl.ds(pl.multiple_of(s * LANES, LANES), LANES)].T
        other = swap(blk)
        half = lane_id(LANES) < 64
        tmp_r[...] = jnp.where(half, blk, other)
        tmp_i[...] = jnp.where(half, other, blk) * sgn
        for v in range(4):
            pup_r[v * 32 : (v + 1) * 32, s, :] = tmp_r[pl.ds(v, 32, stride=4), :]
            pup_i[v * 32 : (v + 1) * 32, s, :] = tmp_i[pl.ds(v, 32, stride=4), :]
        return c

    lax.fori_loop(0, STRIPS, turn, 0)

    src = lax.broadcasted_iota(jnp.int32, (Q, Q), 0)
    dst = lax.broadcasted_iota(jnp.int32, (Q, Q), 1)
    perm[...] = jnp.where(src == 4 * (dst & 127) + (dst >> 7), 1.0, 0.0).astype(BF16)
    for g in range(4):
        root = jnp.sqrt(meas[:, g * Q : (g + 1) * Q])
        high = root.astype(BF16)
        low = (root - high.astype(F32)).astype(BF16)
        moved = jnp.dot(high, perm[...], preferred_element_type=F32) + jnp.dot(low, perm[...], preferred_element_type=F32)
        for q in range(4):
            smq[q, :, g * LANES : (g + 1) * LANES] = moved[:, q * LANES : (q + 1) * LANES]

    fetch[0].wait()

    def shift(e):
        return off[0, led * PER + e] & 127

    def send_plane(b, src, dst, ssem, rsem):
        pltpu.make_async_remote_copy(
            src_ref=src.at[pl.ds(pl.multiple_of(b * 64, 64), 64)],
            dst_ref=dst.at[block],
            send_sem=ssem,
            recv_sem=rsem,
            device_id=plane(b),
            device_id_type=MESH,
        ).start()

    def spread(work, src, dst, ssem, rsem):
        def go(i, own):
            at = (5 * i + block) & 7
            work(at)
            for k in range(1 if own else 0, 4):
                send_plane(at + 8 * ((k + (block >> 3)) & 3), src, dst, ssem, rsem)

        def step(i, c):
            go(i, False)
            return c

        lax.fori_loop(1, 8, step, 0)
        go(8, True)
        pltpu.make_async_copy(src.at[pl.ds(pl.multiple_of(block * 64, 64), 64)], dst.at[block], rsem).start()

    for e in range(PER):
        pltpu.make_async_copy(recv1[e], recv1[e], r1.at[e]).wait()
        delta = shift(e)

        def product(g, c):
            d = 32 * (g & 3) + (g >> 2) + delta
            win = jnp.concatenate([recv1[e][(d + 4 * k) & 127] for k in range(8)], axis=0).astype(F32)
            pr = pup_r[pl.ds(8 * g, 8)].reshape(LANES, LANES)
            pi = pup_i[pl.ds(8 * g, 8)].reshape(LANES, LANES)
            other = swap(win)
            at = pl.multiple_of((g & 3) * LANES, LANES)
            x1[g >> 2, pl.ds(at, LANES), :] = (win * pr + other * pi).astype(BF16)
            x1[g >> 2, pl.ds(at + Q, LANES), :] = ((other * pr - win * pi) * sgn).astype(BF16)
            return c

        lax.fori_loop(0, 16, product, 0, unroll=4)

        def first(v, c):
            ys[v] = jnp.dot(t1[v], x1[v], preferred_element_type=F32)
            return c

        lax.fori_loop(0, 4, first, 0, unroll=4)

        def butterfly(i):
            at = pl.multiple_of(i * 64, 64)
            rows = pl.ds(at, 64)
            y0, y1, y2, y3 = (ys[v, rows, :] for v in range(4))
            even, odd = y0 + y2, y1 + y3
            diff, turned = y0 - y2, swap(y1 - y3) * sgn
            for u, value in enumerate((even + odd, diff + turned, even - odd, diff - turned)):
                send2[e, pl.ds(at + u * Q, 64), :] = value.astype(BF16)

        spread(butterfly, send2.at[e], recv2.at[e], s2.at[e], r2.at[e])

    fetch[1].wait()
    fetch[2].wait()
    for e in range(PER):
        pltpu.make_async_copy(recv2.at[e], recv2.at[e], r2.at[e]).wait()
        for b in range(8):
            a0, a1, a2, a3 = (recv2[e, b + 8 * u].astype(F32) for u in range(4))
            even, odd = a0 + a2, a1 + a3
            diff, turned = a0 - a2, swap(a1 - a3) * sign(b & 1)
            for q, value in enumerate((even + odd, diff + turned, even - odd, diff - turned)):
                xq[q, :, b * LANES : (b + 1) * LANES] = value.astype(BF16)

        def field(q, c):
            got = jnp.dot(xq[q], t2[q], preferred_element_type=F32)
            re, im = got[:, :Q], got[:, Q:]
            factor = 1.0 - smq[q, pl.ds(e * 64, 64), :] * lax.rsqrt(jnp.maximum(re * re + im * im, 0.25))
            rq[q & 1, :, :Q] = (re * factor).astype(BF16)
            rq[q & 1, :, Q:] = (im * factor).astype(BF16)
            zs[q] = jnp.dot(rq[q & 1], t3[q], preferred_element_type=F32)
            return c

        lax.fori_loop(0, 4, field, 0, unroll=2)
        def combine(i):
            lanes = pl.ds(pl.multiple_of(i * LANES, LANES), LANES)
            z0, z1, z2, z3 = (zs[q, :, lanes] for q in range(4))
            even, odd = z0 + z2, z1 + z3
            diff, turned = z0 - z2, swap(z1 - z3) * sign(i & 1)
            for u, value in enumerate((even + odd, diff - turned, even - odd, diff + turned)):
                send3[e, pl.ds(pl.multiple_of(i * 64, 64) + u * Q, 64), :] = value.astype(BF16)

        spread(combine, send3.at[e], recv3.at[e], s3.at[e], r3.at[e])

    fetch[3].wait()
    def along(i):
        return {"band": band, "led": (led + i) & 3, "pencil": pencil}

    for e in range(PER):
        pltpu.make_async_copy(recv3.at[e], recv3.at[e], r3.at[e]).wait()
        delta = shift(e)

        def fold(i, c):
            at = pl.multiple_of(i * 64, 64)
            a0, a1, a2, a3 = (recv3[e, i + 8 * u].astype(F32) for u in range(4))
            b0, b1, b2, b3 = (swap(a) for a in (a0, a1, a2, a3))
            even, odd, diff, turned = a0 + a2, a1 + a3, a0 - a2, (b1 - b3) * sgn
            back_even, back_odd, back_diff, back_turned = b0 + b2, b1 + b3, b0 - b2, (a1 - a3) * sgn
            for q, (value, other) in enumerate((
                (even + odd, back_even + back_odd),
                (diff - turned, back_diff + back_turned),
                (even - odd, back_even - back_odd),
                (diff + turned, back_diff - back_turned),
            )):
                x1[q, pl.ds(at, 64), :] = value.astype(BF16)
                x1[q, pl.ds(at + Q, 64), :] = (other * (-sgn)).astype(BF16)
            return c

        lax.fori_loop(0, 8, fold, 0)

        def last(q, c):
            got = jnp.dot(t4[q], x1[q], preferred_element_type=F32)
            wg[pl.ds(q * 32, 32)] = got.reshape(32, STRIPS, LANES)
            wo[pl.ds(q * 32, 32)] = swap(got).reshape(32, STRIPS, LANES)
            return c

        lax.fori_loop(0, 4, last, 0, unroll=4)

        def pupil_sum(g, c):
            rows = pl.ds(pl.multiple_of(g * LANES, LANES), LANES)
            d = 32 * (g & 3) + (g >> 2) + delta
            win = jnp.concatenate([recv1[e][(d + 4 * k) & 127] for k in range(8)], axis=0).astype(F32)
            grad = wg[pl.ds(8 * g, 8)].reshape(LANES, LANES)
            other = swap(win)
            real = ((lane_id(LANES) >> 6) ^ odd_pencil) == 0
            turned = wo[pl.ds(8 * g, 8)].reshape(LANES, LANES)
            value = grad * jnp.where(real, win, other) - turned * (jnp.where(real, other, win) * sgn)
            if e == 0:
                pg[rows, :] = value
            else:
                value = (value + pg[rows, :]).reshape(8, STRIPS, LANES)
                for k in range(8):
                    pgn[pl.ds(32 * (g & 3) + 4 * k + (g >> 2), STRIPS, stride=LANES), :] = value[k]
            return c

        def narrow(g, c):
            pg16[g >> 1, pl.ds(pl.multiple_of((g & 1) * 256, 256), 256), :] = pgn[
                pl.ds(pl.multiple_of(g * 256, 256), 256), :
            ].astype(BF16)
            return c

        def term(g, own):
            places = [(me + (8 * g + k + 1) * STEP) & 127 for k in range(8)]
            values = []
            for d in places:
                w0 = (d - delta) & 127
                w = (w0 & 3) * 32 + (w0 >> 2)
                values.append((wg[w] * pup_r[w] - wo[w] * pup_i[w]).astype(BF16))
            for d, value in zip(places, values):
                send4[e, d] = value
            for d in places[: 7 if own else 8]:
                pltpu.make_async_remote_copy(
                    src_ref=send4.at[e, d], dst_ref=recv4.at[e, slot_me], send_sem=s4.at[e], recv_sem=r4.at[e],
                    device_id=device(d), device_id_type=MESH,
                ).start()

        def terms(g, c):
            term(g, False)
            return c

        if e > 0:
            lax.fori_loop(0, 16, pupil_sum, 0, unroll=2)
            lax.fori_loop(0, 8, narrow, 0)
            for i in range(1, GROUPS):
                pltpu.make_async_remote_copy(
                    src_ref=pg16.at[(led + i) & 3], dst_ref=rsr.at[led], send_sem=s5.at[i - 1], recv_sem=r5,
                    device_id=along(i), device_id_type=MESH,
                ).start()
        lax.fori_loop(0, 15, terms, 0, unroll=3)
        term(15, True)
        pltpu.make_async_copy(send4.at[e, me], recv4.at[e, slot_me], r4.at[e]).start()
        if e == 0:
            lax.fori_loop(0, 16, pupil_sum, 0, unroll=2)

    pltpu.make_async_copy(rsr.at[pl.ds(0, 3)], rsr.at[pl.ds(0, 3)], r5).wait()
    for k in range(4):
        total = pgn[pl.ds(pl.multiple_of(led * Q + k * LANES, LANES), LANES), :]
        for i in range(1, GROUPS):
            total = total + rsr[(led + i) & 3, k * LANES : (k + 1) * LANES, :].astype(F32)
        total = total.T
        lanes = slice(k * LANES, (k + 1) * LANES)
        agr[led, :64, lanes] = jnp.where(odd_pencil == 0, total[:64], total[64:]).astype(BF16)
        agr[led, 64:, lanes] = jnp.where(odd_pencil == 0, total[64:], total[:64]).astype(BF16)
    for i in range(1, GROUPS):
        pltpu.make_async_remote_copy(
            src_ref=agr.at[led], dst_ref=agr.at[led], send_sem=s6.at[i - 1], recv_sem=r6,
            device_id=along(i), device_id_type=MESH,
        ).start()
    pltpu.make_async_copy(agr.at[pl.ds(0, 3)], agr.at[pl.ds(0, 3)], r6).wait()

    for v in range(4):
        pgout[:, v * Q : (v + 1) * Q] = agr[v].astype(F32)

    for e in range(PER):
        part = pl.ds(0, DEVICES - 1)
        pltpu.make_async_copy(send1.at[e, part], send1.at[e, part], s1.at[e]).wait()
        pltpu.make_async_copy(send4.at[e, part], send4.at[e, part], s4.at[e]).wait()
        pltpu.make_async_copy(recv4.at[e], recv4.at[e], r4.at[e]).wait()
        part = pl.ds(0, W - 64)
        pltpu.make_async_copy(send2.at[e, part], send2.at[e, part], s2.at[e]).wait()
        pltpu.make_async_copy(send3.at[e, part], send3.at[e, part], s3.at[e]).wait()
    for i in range(1, GROUPS):
        pltpu.make_async_copy(pg16.at[0], pg16.at[0], s5.at[i - 1]).wait()
        pltpu.make_async_copy(agr.at[0], agr.at[0], s6.at[i - 1]).wait()


VMEM = pl.BlockSpec(memory_space=pltpu.VMEM)
SMEM = pl.BlockSpec(memory_space=pltpu.SMEM)
ANY = pl.BlockSpec(memory_space=pl.ANY)
HBM = pl.BlockSpec(memory_space=pltpu.HBM)
EXCHANGE = (PER, DEVICES, STRIPS, LANES)


def local(spectrum, pupil, measured, offsets):
    offsets = offsets.T
    small = pltpu.CompilerParams(vmem_limit_bytes=24 << 20)
    rows = spectrum.shape[1]
    tiles = spectrum.shape[3] // LANES
    dma = pltpu.SemaphoreType.DMA
    x = spectrum.reshape(rows, 2, tiles, LANES).transpose(0, 2, 1, 3).reshape(rows, 2 * tiles, LANES)
    send1 = pl.pallas_call(
        cut_kernel,
        out_shape=jax.ShapeDtypeStruct(EXCHANGE, BF16),
        in_specs=[SMEM, VMEM],
        out_specs=VMEM,
        compiler_params=small,
        name="cut",
    )(offsets, x)
    pup = pupil.transpose(0, 2, 1).reshape(LANES, W)
    meas = measured.reshape(PER * 64, W)
    recv4, pgrad = pl.pallas_call(
        core_kernel,
        out_shape=(jax.ShapeDtypeStruct(EXCHANGE, BF16), jax.ShapeDtypeStruct((LANES, W), F32)),
        in_specs=[SMEM, VMEM, VMEM, VMEM, ANY, ANY, ANY, ANY],
        out_specs=(VMEM, VMEM),
        scratch_shapes=[
            pltpu.VMEM((4, Q, 2 * Q), BF16),
            pltpu.VMEM((4, 2 * Q, 2 * Q), BF16),
            pltpu.VMEM((4, 2 * Q, 2 * Q), BF16),
            pltpu.VMEM((4, Q, 2 * Q), BF16),
            pltpu.VMEM(EXCHANGE[1:], BF16),
            pltpu.VMEM(EXCHANGE[1:], BF16),
            pltpu.VMEM((DEVICES, STRIPS, LANES), F32),
            pltpu.VMEM((DEVICES, STRIPS, LANES), F32),
            pltpu.VMEM((LANES, LANES), F32),
            pltpu.VMEM((LANES, LANES), F32),
            pltpu.VMEM((Q, Q), BF16),
            pltpu.VMEM((4, PER * 64, Q), F32),
            pltpu.VMEM((4, 2 * Q, LANES), BF16),
            pltpu.VMEM((4, Q, LANES), F32),
            pltpu.VMEM((PER, W, LANES), BF16),
            pltpu.VMEM((PER, BLOCKS, 64, LANES), BF16),
            pltpu.VMEM((4, 64, 2 * Q), BF16),
            pltpu.VMEM((2, 64, 2 * Q), BF16),
            pltpu.VMEM((4, 64, 2 * Q), F32),
            pltpu.VMEM((PER, W, LANES), BF16),
            pltpu.VMEM((PER, BLOCKS, 64, LANES), BF16),
            pltpu.VMEM((DEVICES, STRIPS, LANES), F32),
            pltpu.VMEM((DEVICES, STRIPS, LANES), F32),
            pltpu.VMEM(EXCHANGE, BF16),
            pltpu.VMEM((W, LANES), F32),
            pltpu.VMEM((W, LANES), F32),
            pltpu.VMEM((4, Q, LANES), BF16),
            pltpu.VMEM((4, Q, LANES), BF16),
            pltpu.VMEM((4, LANES, Q), BF16),
            dma((4,)), dma((PER,)), dma((PER,)), dma((PER,)), dma((PER,)), dma((PER,)), dma((PER,)),
            dma((PER,)), dma((PER,)), dma((3,)), dma, dma((3,)), dma,
        ],
        compiler_params=pltpu.CompilerParams(collective_id=0, has_side_effects=True, vmem_limit_bytes=48 << 20),
        name="core",
    )(offsets, send1, pup, meas, *(jnp.asarray(t) for t in tables()))
    total, pgrad = pl.pallas_call(
        add_kernel,
        out_shape=(jax.ShapeDtypeStruct(x.shape, F32), jax.ShapeDtypeStruct((LANES, W), F32)),
        in_specs=[SMEM, VMEM, VMEM],
        out_specs=(HBM, VMEM),
        scratch_shapes=[pltpu.VMEM((rows, PAD, LANES), F32), pltpu.SMEM((LEDS,), jnp.int32), dma],
        compiler_params=small,
        name="add",
    )(offsets, recv4, pgrad)
    spec_grad = total.reshape(rows, tiles, 2, LANES).transpose(0, 2, 1, 3).reshape(spectrum.shape)
    return spec_grad, pgrad.reshape(2, 64, W).transpose(0, 2, 1)


def solution(mesh):
    return jax.shard_map(
        local,
        mesh=mesh,
        in_specs=(
            P(("band", "led", "pencil"), None, None, None),
            P(None, None, ("band", "pencil")),
            P("led", ("band", "pencil"), None),
            P(),
        ),
        out_specs=(
            P(("band", "led", "pencil"), None, None, None),
            P(None, None, ("band", "pencil")),
        ),
        check_vma=False,
    )
```
